256 devices in a mesh: wave: 64 (over z, y, core), lev: 4 (over x).
Axes of the slice: x: 4, y: 4, z: 8, core: 2. Of those that a mesh axis runs over, the one named last changes fastest.
Arguments:
- fourier: float32 [128, 4, 72, 2560], P(None, None, 'lev', 'wave'), may hold values from -6 to 6
- legendre: float32 [128, 1280, 2560], P('wave', None, 'lev'), may hold values from -0.125 to 0.125
- weights: float32 [2560], replicated, may hold values from 0.25 to 2
- points: int32 [2560], replicated, may hold values from 16 to 3199
- zonal: int32 [128], replicated, may hold values from 0 to 1279, as said below
- pressure_balance_matrix: float32 [72, 72], replicated, may hold values from -0.75 to 0.75
- modes: float32 [72, 72], replicated, may hold values from -0.75 to 0.75
- project: float32 [72, 72], replicated, may hold values from -0.75 to 0.75
- eigen: float32 [72], replicated, may hold values from 0.1 to 10
- thermal_reply_matrix: float32 [72, 72], replicated, may hold values from -0.75 to 0.75
Outputs:
- spectral: float32 [128, 4, 72, 1280], P('wave', None, 'lev')
- fourier_new: float32 [128, 4, 72, 2560], P(None, None, 'lev', 'wave')
The draws below stay inside these ranges and needn't reach their ends.
Inputs may be any that keep to these rules, and one draw needn't show every extreme that they name: Distinct zonal wavenumbers; slot s belongs to wave index s // 2; 0 and 1279 each appear in one slot.
All inputs are finite; a program needn't handle non-finite values.
Results may differ from the reference program's by a relative error of at most 0.000088.
Values sent between devices are 32-bit elements; how exact they have to be, the bound alone decides.
A program may use at most 128 MiB of HBM per device.

```python
import math
import jax
import jax.numpy as jnp
from jax import lax

NN = 1280
LEVELS = 72
LAT = 2560
WAVES = 128


def draw_zonal(key, part):
    key = jax.random.fold_in(key, 11)
    first_key, second_key = jax.random.split(key)
    inner = jax.random.permutation(first_key, NN - 2)[:WAVES - 2].astype(jnp.int32) + 1
    values = jnp.concatenate([jnp.array([0, NN - 1], jnp.int32), inner])
    return jax.random.permutation(second_key, values).astype(jnp.int32)


def with_ends(values, key, low, high):
    shape = values.shape
    place = [jax.random.randint(jax.random.fold_in(key, axis), (), 0, shape[axis]) for axis in range(len(shape))]
    values = values.at[tuple(place)].set(low)
    longest = shape.index(max(shape))
    place[longest] = (place[longest] + 1) % shape[longest]
    return values.at[tuple(place)].set(high)


def shard_levels(rng, shape, pieces, smallest, high):
    gain, own = 1.0, jax.random.fold_in(rng, 6)
    for axis_at, shards_of in pieces:
        heights = jnp.exp(jax.random.uniform(jax.random.fold_in(own, axis_at), (shards_of,), jnp.float32, smallest / len(pieces), high / len(pieces)))
        gain = gain * jnp.repeat(heights, shape[axis_at] // shards_of).reshape([-1 if axis == axis_at else 1 for axis in range(len(shape))])
    return gain


def noise(key, extent, deviation, reach, cuts=(), kind=jnp.bfloat16):
    factor_of = shard_levels(key, extent, cuts, -0.22, 0.18) if cuts else 1.0
    result = jax.random.normal(key, extent, jnp.float32) * deviation * factor_of
    return jnp.minimum(jnp.maximum(result, -reach), reach).astype(kind)


def setup_inputs(seed: int = 0) -> dict:
    key_list = jax.random.split(jax.random.key(seed), 11)
    fourier = noise(key_list[0], (WAVES, 4, LEVELS, LAT), 1.0, 6.0, ((2, 4), (3, 64)), jnp.float32)
    legendre = noise(key_list[1], (WAVES, NN, LAT), LAT ** -0.5, 0.125, ((0, 64), (2, 4)), jnp.float32)
    weights = jnp.clip(jnp.exp(jax.random.uniform(key_list[2], (LAT,), jnp.float32, math.log(0.25), math.log(2.0))), 0.25, 2.0)
    points = with_ends(jax.random.randint(key_list[3], (LAT,), 16, 2 * NN + NN // 2), jax.random.fold_in(key_list[3], 1), 16, (2 * NN + NN // 2) - 1).astype(jnp.int32)
    zonal = draw_zonal(jax.random.fold_in(key_list[10], 71), 0)
    pressure_balance_matrix = noise(key_list[5], (LEVELS, LEVELS), LEVELS ** -0.5, 0.75, (), jnp.float32)
    modes = noise(key_list[6], (LEVELS, LEVELS), LEVELS ** -0.5, 0.75, (), jnp.float32)
    project = noise(key_list[7], (LEVELS, LEVELS), LEVELS ** -0.5, 0.75, (), jnp.float32)
    eigen = jnp.clip(jnp.exp(jax.random.uniform(key_list[8], (LEVELS,), jnp.float32, math.log(0.1), math.log(10.0))), 0.1, 10.0)
    thermal_reply_matrix = noise(key_list[9], (LEVELS, LEVELS), LEVELS ** -0.5, 0.75, (), jnp.float32)
    return {"fourier": fourier, "legendre": legendre, "weights": weights, "points": points, "zonal": zonal, "pressure_balance_matrix": pressure_balance_matrix, "modes": modes, "project": project, "eigen": eigen, "thermal_reply_matrix": thermal_reply_matrix}


def helmholtz(harmonic_amplitudes, pressure_balance_matrix, modes, project, eigen, thermal_reply_matrix, total):
    highest = lax.Precision.HIGHEST
    wavenumber = jnp.arange(total, dtype=jnp.int32)
    timestep_weighting = (wavenumber * (wavenumber + 1)).astype(jnp.float32) * (4.0 / (total * (total + 1)))
    velocity_spreading = harmonic_amplitudes[:, 0:2]
    thermal_state = harmonic_amplitudes[:, 2:4]
    tendency_sources = velocity_spreading + timestep_weighting * jnp.einsum('kl,mcln->mckn', pressure_balance_matrix, thermal_state, precision=highest)
    modal = jnp.einsum('kl,mcln->mckn', project, tendency_sources, precision=highest) / (1.0 + eigen[:, None] * timestep_weighting)
    revised_spreading = jnp.einsum('kl,mcln->mckn', modes, modal, precision=highest)
    revised_thermal = thermal_state - jnp.einsum('kl,mcln->mckn', thermal_reply_matrix, revised_spreading, precision=highest)
    return jnp.concatenate([revised_spreading, revised_thermal], axis=1)


def reference(fourier, legendre, weights, points, zonal, pressure_balance_matrix, modes, project, eigen, thermal_reply_matrix):
    highest = lax.Precision.HIGHEST
    present = (2 * zonal[:, None] < points[None, :])[:, None, None, :]
    scaled = jnp.where(present, fourier, 0.0) * weights
    harmonic_amplitudes = jnp.einsum('mclj,mnj->mcln', scaled, legendre, precision=highest)
    wavenumber = jnp.arange(NN, dtype=jnp.int32)
    living = (wavenumber[None, :] >= zonal[:, None])[:, None, None, :]
    harmonic_amplitudes = jnp.where(living, harmonic_amplitudes, 0.0)
    spectral = helmholtz(harmonic_amplitudes, pressure_balance_matrix, modes, project, eigen, thermal_reply_matrix, NN)
    synthesis = jnp.einsum('mcln,mnj->mclj', spectral, legendre, precision=highest)
    fourier_new = jnp.where(present, synthesis, 0.0)
    return spectral, fourier_new
```

```python
import functools

import jax
import jax.numpy as jnp
import numpy as np
from jax import lax
from jax.experimental import pallas as pl
from jax.experimental.pallas import tpu as pltpu
from jax.sharding import PartitionSpec as P

MESH = pl.DeviceIdType.MESH
LANES = 128


def kernel(
    dims,
    fourier,
    legendre,
    weights,
    points,
    zonal,
    zonal_row,
    balance,
    modes,
    project,
    eigen,
    reply,
    pick_div,
    pick_temp,
    place_div,
    place_temp,
    spectral,
    fourier_new,
    leg_full,
    leg_hi,
    leg_lo,
    mask_weight,
    mask_present,
    square,
    out_rows,
    in_rows,
    relay_a,
    relay_b,
    blocks,
    planes,
    grid_hi,
    grid_lo,
    partial,
    sum_a,
    sum_b,
    sum_left,
    sum_right,
    modal_in,
    modal_out,
    solved,
    mixed,
    spec_hi,
    spec_lo,
    packed,
    returned,
    final_rows,
    leg_sem,
    wave_send,
    wave_recv,
    lev_send,
    lev_recv,
    relay_recv,
    sum_send,
    sum_recv,
    gather_send,
    gather_recv,
    local_sem,
):
    nw, nx, band, lev, total, quarter = dims
    per = LANES // band
    groups = 4 * lev // per
    unit = (nw // nx) * groups
    half_unit = unit // 2
    rows = 2 * nx * lev
    half_rows = rows // 2
    tiles_j = quarter // LANES
    tiles_n = total // LANES
    half_n = total // 2
    highest = lax.Precision.HIGHEST
    f32, bf16 = jnp.float32, jnp.bfloat16
    w = lax.axis_index("wave")
    x = lax.axis_index("lev")
    right, left, far = lax.rem(x + 1, nx), lax.rem(x + nx - 1, nx), lax.rem(x + 2, nx)

    def remote(src, dst, send, recv, to_w, to_x):
        return pltpu.make_async_remote_copy(
            src_ref=src,
            dst_ref=dst,
            send_sem=send,
            recv_sem=recv,
            device_id=(to_w, to_x),
            device_id_type=MESH,
        )

    def drain(ref, sem):
        pltpu.make_async_copy(ref, ref, sem).wait()

    leg_copies = [
        pltpu.make_async_copy(legendre.at[s], leg_full.at[s], leg_sem.at[s])
        for s in range(2)
    ]
    for copy in leg_copies:
        copy.start()

    barrier = pltpu.get_barrier_semaphore()

    @pl.loop(1, nw)
    def _(k):
        pl.semaphore_signal(
            barrier, inc=1, device_id=(lax.rem(w + k, nw), x), device_id_type=MESH
        )

    for k in range(1, nx):
        pl.semaphore_signal(
            barrier, inc=1, device_id=(w, lax.rem(x + k, nx)), device_id_type=MESH
        )

    twice = 2 * zonal_row[...]
    for j in range(band):
        here = twice < points[w * band + j]
        mask_weight[j : j + 1, :] = jnp.where(here, weights[w * band + j], 0.0)
        mask_present[j : j + 1, :] = jnp.where(here, 1.0, 0.0)

    def first_row(g):
        pair, r = g // 2, g % 2
        c, third = pair // (lev // per), pair % (lev // per)
        return pl.multiple_of(((2 * c + r) * lev + per * third) * band, 8)

    @pl.loop(0, groups)
    def _(g):
        block = fourier[pl.ds(first_row(g), per * band), :]
        block = (block.reshape(per, band, LANES) * mask_weight[...][None]).reshape(
            per * band, LANES
        )
        block = jnp.concatenate(
            [block, jnp.zeros((LANES - per * band, LANES), f32)], axis=0
        )
        out_rows[pl.ds(g, 2 * nw, stride=groups), :] = block.T

    pl.semaphore_wait(barrier, nw - 1 + nx - 1)

    def wave_exchange(s, kind, source, target):
        @pl.loop(1, nw)
        def _(k):
            to = lax.rem(w + k, nw)
            remote(
                source(to), target(w), wave_send.at[kind, s], wave_recv.at[kind, s], to, x
            ).start()

        pltpu.make_async_copy(source(w), target(w), wave_recv.at[kind, s]).start()

    def wave_in(s):
        wave_exchange(
            s,
            0,
            lambda to: out_rows.at[
                pl.ds(pl.multiple_of((2 * to + s) * groups, 8), groups), :
            ],
            lambda me: in_rows.at[s, pl.ds(pl.multiple_of(me * groups, 8), groups), :],
        )

    def wave_out(s):
        wave_exchange(
            s,
            1,
            lambda to: returned.at[s, pl.ds(pl.multiple_of(to * groups, 8), groups), :],
            lambda me: final_rows.at[s, pl.ds(pl.multiple_of(me * groups, 8), groups), :],
        )

    def span(q, start=0, size=unit):
        return pl.ds(pl.multiple_of(q * unit + start, 8), size)

    def lev_start(s, kind, source, target):
        send, recv = lev_send.at[kind, s], lev_recv.at[kind, s]
        remote(
            source.at[s, span(far, 0, half_unit), :],
            relay_a.at[kind, s],
            send,
            relay_recv.at[kind, s, 0],
            w,
            right,
        ).start()
        remote(
            source.at[s, span(far, half_unit, half_unit), :],
            relay_b.at[kind, s],
            send,
            relay_recv.at[kind, s, 1],
            w,
            left,
        ).start()
        for to in (right, left):
            remote(
                source.at[s, span(to), :], target.at[s, span(x), :], send, recv, w, to
            ).start()
        pltpu.make_async_copy(
            source.at[s, span(x), :], target.at[s, span(x), :], recv
        ).start()

    def lev_forward(s, kind, target):
        send, recv = lev_send.at[kind, s], lev_recv.at[kind, s]
        drain(relay_a.at[kind, s], relay_recv.at[kind, s, 0])
        remote(
            relay_a.at[kind, s],
            target.at[s, span(left, 0, half_unit), :],
            send,
            recv,
            w,
            right,
        ).start()
        drain(relay_b.at[kind, s], relay_recv.at[kind, s, 1])
        remote(
            relay_b.at[kind, s],
            target.at[s, span(right, half_unit, half_unit), :],
            send,
            recv,
            w,
            left,
        ).start()

    def lev_wait(s, kind, target):
        drain(target.at[s], lev_recv.at[kind, s])

    lane = lax.broadcasted_iota(jnp.int32, (groups, LANES), 1)

    def unpack(s):
        @pl.loop(0, nx)
        def _(lg):
            base = lg * unit
            bands = [
                blocks[s, pl.ds(pl.multiple_of(base + b * groups, 8), groups), :]
                for b in range(nw // nx)
            ]
            for i in range(per):
                at = pl.ds(pl.multiple_of((lg * per + i) * groups, 8), groups)
                for t in range(tiles_j):
                    value = None
                    for b in range(nw // nx):
                        low = b * band - t * LANES
                        if low + band <= 0 or low >= LANES:
                            continue
                        turn = (low - i * band) % LANES
                        moved = pltpu.roll(bands[b], turn, 1) if turn else bands[b]
                        value = moved if value is None else jnp.where(lane >= low, moved, value)
                    planes[t, at, :] = value
        for t in range(tiles_j):
            for r in range(2):
                value = planes[t, pl.ds(r, rows, stride=2), :]
                high = value.astype(bf16)
                grid_hi[r * rows : (r + 1) * rows, t * LANES : (t + 1) * LANES] = high
                grid_lo[r * rows : (r + 1) * rows, t * LANES : (t + 1) * LANES] = (
                    value - high.astype(f32)
                ).astype(bf16)

    def analysis(s, q):
        r, part = q // 2, q % 2
        at = pl.ds(pl.multiple_of(r * rows, 16), rows)
        a_hi, a_lo = grid_hi[at, :], grid_lo[at, :]
        n_at = pl.ds(pl.multiple_of(part * half_n, 16), half_n)
        b_hi, b_lo = leg_hi[s, n_at, :], leg_lo[s, n_at, :]
        dot = functools.partial(
            lax.dot_general,
            dimension_numbers=(((1,), (1,)), ((), ())),
            preferred_element_type=f32,
        )
        partial[s, q] = dot(a_hi, b_hi) + (dot(a_hi, b_lo) + dot(a_lo, b_hi))

    top, bottom = pl.ds(0, half_rows), pl.ds(half_rows, half_rows)

    def reduce_start(s):
        send = sum_send.at[s]
        analysis(s, far)
        remote(
            partial.at[s, far, top], sum_a.at[s], send, sum_recv.at[s, 0], w, right
        ).start()
        remote(
            partial.at[s, far, bottom], sum_b.at[s], send, sum_recv.at[s, 1], w, left
        ).start()
        analysis(s, right)
        remote(
            partial.at[s, right, bottom],
            sum_left.at[s, bottom],
            send,
            sum_recv.at[s, 2],
            w,
            right,
        ).start()
        analysis(s, left)
        remote(
            partial.at[s, left, top],
            sum_right.at[s, top],
            send,
            sum_recv.at[s, 3],
            w,
            left,
        ).start()
        analysis(s, x)

    def reduce_forward(s):
        send = sum_send.at[s]
        drain(sum_a.at[s], sum_recv.at[s, 0])
        partial[s, right, top, :] += sum_a[s]
        remote(
            partial.at[s, right, top],
            sum_left.at[s, top],
            send,
            sum_recv.at[s, 4],
            w,
            right,
        ).start()
        drain(sum_b.at[s], sum_recv.at[s, 1])
        partial[s, left, bottom, :] += sum_b[s]
        remote(
            partial.at[s, left, bottom],
            sum_right.at[s, bottom],
            send,
            sum_recv.at[s, 5],
            w,
            left,
        ).start()

    def solve(s):
        drain(sum_left.at[s, bottom], sum_recv.at[s, 2])
        drain(sum_right.at[s, top], sum_recv.at[s, 3])
        drain(sum_left.at[s, top], sum_recv.at[s, 4])
        drain(sum_right.at[s, bottom], sum_recv.at[s, 5])
        value = partial[s, x] + (sum_left[s] + sum_right[s])
        n = lax.broadcasted_iota(jnp.int32, (1, half_n), 1) + (x % 2) * half_n
        value = jnp.where(n >= zonal[2 * w + s], value, 0.0)
        factor = (n * (n + 1)).astype(f32) * (4.0 / (total * (total + 1)))
        size = nx * lev
        both = jnp.dot(modal_in[...], value, precision=highest, preferred_element_type=f32)
        diagonal = lax.broadcasted_iota(jnp.int32, (size, size), 0) == lax.broadcasted_iota(
            jnp.int32, (size, size), 1
        )
        depth = jnp.sum(jnp.where(diagonal, eigen[...], 0.0), axis=1, keepdims=True)
        modal = (both[:size] + factor * both[size:]) / (1.0 + depth * factor)
        answer = jnp.dot(modal_out[...], modal, precision=highest, preferred_element_type=f32)
        row = lax.broadcasted_iota(jnp.int32, (rows, 1), 0)
        thermal = (row // (lev // per)) % 2 == 1
        solved[s, x] = answer + jnp.where(thermal, value, 0.0)

    def gather_start(s):
        send = gather_send.at[s]
        for to, first in ((right, 0), (left, 1)):
            for part in (first, 1 - first):
                at = (top, bottom)[part]
                remote(
                    solved.at[s, x, at],
                    solved.at[s, x, at],
                    send,
                    gather_recv.at[s, 2 * first + part],
                    w,
                    to,
                ).start()

    def gather_forward(s):
        send = gather_send.at[s]
        drain(solved.at[s, left, top], gather_recv.at[s, 0])
        remote(
            solved.at[s, left, top],
            solved.at[s, left, top],
            send,
            gather_recv.at[s, 4],
            w,
            right,
        ).start()
        drain(solved.at[s, right, bottom], gather_recv.at[s, 3])
        remote(
            solved.at[s, right, bottom],
            solved.at[s, right, bottom],
            send,
            gather_recv.at[s, 5],
            w,
            left,
        ).start()

    def gather_wait(s):
        drain(solved.at[s, left, bottom], gather_recv.at[s, 1])
        drain(solved.at[s, right, top], gather_recv.at[s, 2])
        drain(solved.at[s, far, top], gather_recv.at[s, 4])
        drain(solved.at[s, far, bottom], gather_recv.at[s, 5])

    def synthesis(s):
        for r in range(2):
            for t in range(tiles_n):
                part, inner = t // (tiles_n // 2), t % (tiles_n // 2)
                mixed[t, pl.ds(r, rows, stride=2), :] = solved[
                    s, 2 * r + part, :, inner * LANES : (inner + 1) * LANES
                ]
        for t in range(tiles_n):
            value = mixed[t]
            high = value.astype(bf16)
            spec_hi[:, t * LANES : (t + 1) * LANES] = high
            spec_lo[:, t * LANES : (t + 1) * LANES] = (value - high.astype(f32)).astype(bf16)
        start = 0
        while start < quarter:
            size = min(256, quarter - start)
            b_hi = leg_hi[s, :, start : start + size]
            b_lo = leg_lo[s, :, start : start + size]
            dot = functools.partial(jnp.dot, preferred_element_type=f32)
            value = dot(spec_hi[...], b_hi) + (
                dot(spec_hi[...], b_lo) + dot(spec_lo[...], b_hi)
            )
            for t in range(size // LANES):
                planes[start // LANES + t] = value[:, t * LANES : (t + 1) * LANES]
            start += size

    def write_spectral(s):
        thirds = lev // per
        for t in range(tiles_n):
            for i in range(per):
                for c in range(2):
                    for r in range(2):
                        value = mixed[
                            t,
                            pl.ds(x * per * groups + groups * i + 2 * thirds * c + r, thirds, stride=2),
                            :,
                        ]
                        spectral[
                            s, t, pl.ds(4 * i + 2 * c + r, thirds, stride=4 * per), :
                        ] = value

    def pack(s):
        @pl.loop(0, nx)
        def _(lg):
            for b in range(nw // nx):
                value = None
                for i in range(per):
                    at = pl.ds(pl.multiple_of((lg * per + i) * groups, 8), groups)
                    t, low = (b * band) // LANES, (b * band) % LANES
                    turn = (i * band - low) % LANES
                    source = planes[t, at, :]
                    moved = pltpu.roll(source, turn, 1) if turn else source
                    if low + band > LANES:
                        other = planes[t + 1, at, :]
                        other = pltpu.roll(other, turn, 1) if turn else other
                        moved = jnp.where(lane >= i * band + LANES - low, other, moved)
                    value = moved if value is None else jnp.where(lane >= i * band, moved, value)
                packed[s, pl.ds(pl.multiple_of(lg * unit + b * groups, 8), groups), :] = value

    wave_in(0)
    wave_in(1)

    chunk = 64
    for s in range(2):
        leg_copies[s].wait()

        @pl.loop(0, total // chunk)
        def _(k):
            at = pl.ds(pl.multiple_of(k * chunk, chunk), chunk)
            value = leg_full[s, at, :]
            high = value.astype(bf16)
            leg_hi[s, at, :] = high
            leg_lo[s, at, :] = (value - high.astype(f32)).astype(bf16)

    exact = functools.partial(jnp.dot, precision=highest, preferred_element_type=f32)
    size = nx * lev
    modal_in[:size, :] = exact(project[...], pick_div[...])
    modal_in[size:, :] = exact(exact(project[...], balance[...]), pick_temp[...])
    modal_out[...] = exact(place_div[...], modes[...]) - exact(
        place_temp[...], exact(reply[...], modes[...])
    )

    drain(in_rows.at[0], wave_recv.at[0, 0])
    lev_start(0, 0, in_rows, blocks)
    lev_forward(0, 0, blocks)
    lev_wait(0, 0, blocks)
    unpack(0)
    reduce_start(0)
    drain(in_rows.at[1], wave_recv.at[0, 1])
    lev_start(1, 0, in_rows, blocks)
    reduce_forward(0)
    lev_forward(1, 0, blocks)
    solve(0)
    gather_start(0)
    lev_wait(1, 0, blocks)
    unpack(1)
    gather_forward(0)
    reduce_start(1)
    gather_wait(0)
    reduce_forward(1)
    synthesis(0)
    pack(0)
    lev_start(0, 1, packed, returned)
    solve(1)
    gather_start(1)
    lev_forward(0, 1, returned)
    write_spectral(0)
    gather_forward(1)
    lev_wait(0, 1, returned)
    wave_out(0)
    gather_wait(1)
    synthesis(1)
    pack(1)
    lev_start(1, 1, packed, returned)
    write_spectral(1)
    lev_forward(1, 1, returned)
    lev_wait(1, 1, returned)
    wave_out(1)

    sent = (nw - 1) * groups
    for s in range(2):
        for kind in range(2):
            drain(in_rows.at[s, pl.ds(0, sent), :], wave_send.at[kind, s])
            drain(blocks.at[s], lev_send.at[kind, s])
        drain(solved.at[s, pl.ds(0, 3)], sum_send.at[s])
        drain(solved.at[s, pl.ds(0, 3)], gather_send.at[s])
    for s in range(2):
        drain(final_rows.at[s], wave_recv.at[1, s])

    present = mask_present[...] > 0.5

    @pl.loop(0, groups)
    def _(g):
        for s in range(2):
            square[pl.ds(s, nw, stride=2), :] = final_rows[s, pl.ds(g, nw, stride=groups), :]
        block = square[...].T[: per * band].reshape(per, band, LANES)
        block = jnp.where(present[None], block, 0.0).reshape(per * band, LANES)
        fourier_new[pl.ds(first_row(g), per * band), :] = block


def on_device(
    nw,
    nx,
    fourier,
    legendre,
    weights,
    points,
    zonal,
    pressure_balance_matrix,
    modes,
    project,
    eigen,
    thermal_reply_matrix,
):
    waves, parts, lev, band = fourier.shape
    slots, total, quarter = legendre.shape
    size = nx * lev
    per = LANES // band
    groups = parts * lev // per
    unit = (nw // nx) * groups
    rows = 2 * size
    half_n = total // 2
    dims = (nw, nx, band, lev, total, quarter)

    pick = np.zeros((2, size, rows), np.float32)
    row = 0
    for group in range(nx):
        for i in range(per):
            for c in range(2):
                for third in range(lev // per):
                    pick[c, group * lev + per * third + i, row] = 1.0
                    row += 1

    view = fourier.transpose(1, 2, 3, 0).reshape(parts * lev * band, waves)
    f32, bf16 = jnp.float32, jnp.bfloat16
    vmem = pl.BlockSpec(memory_space=pltpu.VMEM)
    smem = pl.BlockSpec(memory_space=pltpu.SMEM)
    dma = pltpu.SemaphoreType.DMA
    spectral, fourier_new = pl.pallas_call(
        functools.partial(kernel, dims),
        out_shape=(
            jax.ShapeDtypeStruct((slots, total // LANES, parts * lev, LANES), f32),
            jax.ShapeDtypeStruct(view.shape, f32),
        ),
        in_specs=[vmem, pl.BlockSpec(memory_space=pl.ANY), smem, smem, smem] + [vmem] * 10,
        out_specs=(vmem, vmem),
        scratch_shapes=[
            pltpu.VMEM((slots, total, quarter), f32),
            pltpu.VMEM((slots, total, quarter), bf16),
            pltpu.VMEM((slots, total, quarter), bf16),
            pltpu.VMEM((band, LANES), f32),
            pltpu.VMEM((band, LANES), f32),
            pltpu.VMEM((LANES, LANES), f32),
            pltpu.VMEM((waves * groups, LANES), f32),
            pltpu.VMEM((slots, nw * groups, LANES), f32),
            pltpu.VMEM((2, slots, unit // 2, LANES), f32),
            pltpu.VMEM((2, slots, unit // 2, LANES), f32),
            pltpu.VMEM((slots, nx * unit, LANES), f32),
            pltpu.VMEM((quarter // LANES, 2 * rows, LANES), f32),
            pltpu.VMEM((2 * rows, quarter), bf16),
            pltpu.VMEM((2 * rows, quarter), bf16),
            pltpu.VMEM((slots, 4, rows, half_n), f32),
            pltpu.VMEM((slots, rows // 2, half_n), f32),
            pltpu.VMEM((slots, rows // 2, half_n), f32),
            pltpu.VMEM((slots, rows, half_n), f32),
            pltpu.VMEM((slots, rows, half_n), f32),
            pltpu.VMEM((rows, rows), f32),
            pltpu.VMEM((rows, size), f32),
            pltpu.VMEM((slots, 4, rows, half_n), f32),
            pltpu.VMEM((total // LANES, 2 * rows, LANES), f32),
            pltpu.VMEM((2 * rows, total), bf16),
            pltpu.VMEM((2 * rows, total), bf16),
            pltpu.VMEM((slots, nx * unit, LANES), f32),
            pltpu.VMEM((slots, nx * unit, LANES), f32),
            pltpu.VMEM((slots, nw * groups, LANES), f32),
            dma((2,)),
            dma((2, 2)),
            dma((2, 2)),
            dma((2, 2)),
            dma((2, 2)),
            dma((2, 2, 2)),
            dma((2,)),
            dma((2, 6)),
            dma((2,)),
            dma((2, 6)),
            dma((1,)),
        ],
        compiler_params=pltpu.CompilerParams(
            collective_id=0, has_side_effects=True, vmem_limit_bytes=58 * 1024 * 1024
        ),
    )(
        view,
        legendre,
        weights,
        points,
        zonal,
        zonal.reshape(1, waves),
        pressure_balance_matrix,
        modes,
        project,
        eigen.reshape(1, size),
        thermal_reply_matrix,
        jnp.asarray(pick[0]),
        jnp.asarray(pick[1]),
        jnp.asarray(pick[0].T),
        jnp.asarray(pick[1].T),
    )
    spectral = (
        spectral.reshape(slots, total // LANES, lev, parts, LANES)
        .transpose(0, 3, 2, 1, 4)
        .reshape(slots, parts, lev, total)
    )
    fourier_new = fourier_new.reshape(parts, lev, band, waves).transpose(3, 0, 1, 2)
    return (spectral, fourier_new)


def solution(mesh):
    return jax.shard_map(
        functools.partial(on_device, mesh.shape["wave"], mesh.shape["lev"]),
        mesh=mesh,
        in_specs=(
            P(None, None, "lev", "wave"),
            P("wave", None, "lev"),
            P(),
            P(),
            P(),
            P(),
            P(),
            P(),
            P(),
            P(),
        ),
        out_specs=(P("wave", None, "lev", None), P(None, None, "lev", "wave")),
        check_vma=False,
    )
```

```python
import functools

import jax
import jax.numpy as jnp
import numpy as np
from jax import lax
from jax.experimental import pallas as pl
from jax.experimental.pallas import tpu as pltpu
from jax.sharding import PartitionSpec as P

MESH = pl.DeviceIdType.MESH
LANES = 128
CHUNKS_IN = (((0, 8), (8, 8), (16, 8)), ((0, 8), (8, 8), (16, 8)))
CHUNKS_OUT = (((0, 8), (8, 8), (16, 8)), ((0, 8), (8, 8), (16, 8)))


def kernel(
    dims,
    fourier,
    legendre,
    weights,
    points,
    zonal,
    zonal_row,
    balance,
    modes,
    project,
    eigen,
    reply,
    pick_div,
    pick_temp,
    place_div,
    place_temp,
    spectral,
    fourier_new,
    leg_full,
    leg_hi,
    leg_lo,
    mask_weight,
    mask_present,
    square,
    out_rows,
    in_rows,
    blocks,
    planes_in,
    planes_out,
    grid_hi,
    grid_lo,
    partial,
    sum_a,
    sum_b,
    sum_left,
    sum_right,
    modal_in,
    modal_out,
    solved,
    mixed,
    spec_hi,
    spec_lo,
    spec_rows,
    packed,
    returned,
    final,
    result,
    leg_sem,
    wave_send,
    wave_recv,
    lev_send,
    lev_recv,
    sum_send,
    sum_recv,
    gather_send,
    gather_recv,
    out_sem,
):
    nw, nx, band, lev, total, quarter = dims
    per = LANES // band
    thirds = lev // per
    pairs = 2 * thirds
    cells = nx * per
    groups = 2 * pairs
    near = nw // nx
    size = nx * lev
    rows = 2 * size
    tiles_j = quarter // LANES
    tiles_n = total // LANES
    half_n = total // 2
    half = LANES // 2
    whole = 2 * rows + size
    highest = lax.Precision.HIGHEST
    f32, bf16 = jnp.float32, jnp.bfloat16
    w = lax.axis_index("wave")
    x = lax.axis_index("lev")
    right, left, far = lax.rem(x + 1, nx), lax.rem(x + nx - 1, nx), lax.rem(x + 2, nx)
    chunks = (CHUNKS_IN, CHUNKS_OUT)

    def remote(src, dst, send, recv, to_w, to_x):
        return pltpu.make_async_remote_copy(
            src_ref=src,
            dst_ref=dst,
            send_sem=send,
            recv_sem=recv,
            device_id=(to_w, to_x),
            device_id_type=MESH,
        )

    def drain(ref, sem):
        pltpu.make_async_copy(ref, ref, sem).wait()

    leg_copies = [
        pltpu.make_async_copy(legendre.at[s], leg_full.at[s], leg_sem.at[s])
        for s in range(2)
    ]
    for copy in leg_copies:
        copy.start()

    barrier = pltpu.get_barrier_semaphore()

    @pl.loop(1, nw)
    def _(k):
        pl.semaphore_signal(
            barrier, inc=1, device_id=(lax.rem(w + k, nw), x), device_id_type=MESH
        )

    for k in range(1, nx):
        pl.semaphore_signal(
            barrier, inc=1, device_id=(w, lax.rem(x + k, nx)), device_id_type=MESH
        )

    twice = 2 * zonal_row[...]
    for j in range(band):
        here = twice < points[w * band + j]
        mask_weight[j : j + 1, :] = jnp.where(here, weights[w * band + j], 0.0)
        mask_present[j : j + 1, :] = jnp.where(here, 1.0, 0.0)

    def first_row(r, k):
        c, third = k // thirds, k % thirds
        return pl.multiple_of(((2 * c + r) * lev + per * third) * band, 8)

    def spread(r):
        @pl.loop(0, pairs)
        def _(k):
            block = fourier[pl.ds(first_row(r, k), per * band), :]
            block = (block.reshape(per, band, LANES) * mask_weight[...][None]).reshape(
                per * band, LANES
            )
            block = jnp.concatenate(
                [block, jnp.zeros((LANES - per * band, LANES), f32)], axis=0
            )
            out_rows[r, pl.ds(k, 2 * nw, stride=pairs), :] = block.T

    def from_wave(index, chunk):
        first, n = chunk
        return pl.ds(pl.multiple_of(nw * first + index * n, 8), n)

    def all_waves(chunk, count=nw):
        first, n = chunk
        return pl.ds(nw * first, count * n)

    def wave_exchange(kind, r, c, source, target):
        send, recv = wave_send.at[kind, r, c], wave_recv.at[kind, r, c]

        @pl.loop(1, nw)
        def _(k):
            to = lax.rem(w + k, nw)
            remote(source(to), target, send, recv, to, x).start()

        pltpu.make_async_copy(source(w), target, recv).start()

    def wave_in(r, c):
        chunk = chunks[0][r][c]
        first, n = chunk
        wave_exchange(
            0,
            r,
            c,
            lambda to: out_rows.at[r, pl.ds(pl.multiple_of(to * groups + first, 8), n), :],
            in_rows.at[r, from_wave(w, chunk), :],
        )

    def wave_in_wait(r, c):
        drain(in_rows.at[r, all_waves(chunks[0][r][c]), :], wave_recv.at[0, r, c])

    def wave_out(r, c):
        chunk = chunks[1][r][c]
        wave_exchange(
            1,
            r,
            c,
            lambda to: returned.at[r, from_wave(to, chunk), :],
            final.at[r, from_wave(w, chunk), :],
        )

    def wave_out_wait(r, c):
        drain(final.at[r, all_waves(chunks[1][r][c]), :], wave_recv.at[1, r, c])

    def span(q, chunk):
        first, n = chunk
        return pl.ds(pl.multiple_of(nw * first + q * (near * n), 8), near * n)

    def lev_start(kind, r, c):
        source, target = ((in_rows, blocks), (packed, returned))[kind]
        chunk = chunks[kind][r][c]
        send, recv = lev_send.at[kind, r, c], lev_recv.at[kind, r, c]
        for to in (far, right, left):
            remote(
                source.at[r, span(to, chunk), :],
                target.at[r, span(x, chunk), :],
                send,
                recv,
                w,
                to,
            ).start()
        pltpu.make_async_copy(
            source.at[r, span(x, chunk), :], target.at[r, span(x, chunk), :], recv
        ).start()

    def lev_wait(kind, r, c):
        target = (blocks, returned)[kind]
        drain(target.at[r, all_waves(chunks[kind][r][c]), :], lev_recv.at[kind, r, c])

    def unpack(r, c):
        chunk = chunks[0][r][c]
        first, n = chunk
        lane = lax.broadcasted_iota(jnp.int32, (n, LANES), 1)

        @pl.loop(0, nx)
        def _(lg):
            bands = [
                blocks[r, from_wave(lg * near + b, chunk), :]
                for b in range(near)
            ]
            for i in range(per):
                at = pl.ds(first * cells + lg * per + i, n, stride=cells)
                for t in range(tiles_j):
                    value = None
                    for b in range(near):
                        low = b * band - t * LANES
                        if low + band <= 0 or low >= LANES:
                            continue
                        turn = (low - i * band) % LANES
                        moved = pltpu.roll(bands[b], turn, 1) if turn else bands[b]
                        value = moved if value is None else jnp.where(lane >= low, moved, value)
                    planes_in[t, at, :] = value

    def analysis(p, h):
        s = p % 2
        n_at = pl.ds(pl.multiple_of(h * half_n, 16), half_n)
        b_hi, b_lo = leg_hi[s, n_at, :], leg_lo[s, n_at, :]
        dot = functools.partial(
            lax.dot_general,
            dimension_numbers=(((1,), (1,)), ((), ())),
            preferred_element_type=f32,
        )
        value = dot(grid_hi[...], b_hi) + (
            dot(grid_hi[...], b_lo) + dot(grid_lo[...], b_hi)
        )
        low = lax.broadcasted_iota(jnp.int32, (size, LANES), 1) < half
        even, odd = 2 * h, 2 * h + 1
        partial[p, even, 0:rows, :] = value[:, 0:LANES]
        partial[p, even, rows : 2 * rows, :] = value[:, LANES : 2 * LANES]
        middle = value[:, 2 * LANES : 3 * LANES]
        first, second = middle[:size], middle[size:]
        partial[p, even, 2 * rows :, :] = jnp.where(low, first, pltpu.roll(second, half, 1))
        partial[p, odd, 2 * rows :, :] = jnp.where(low, pltpu.roll(first, half, 1), second)
        partial[p, odd, 0:rows, :] = value[:, 3 * LANES : 4 * LANES]
        partial[p, odd, rows : 2 * rows, :] = value[:, 4 * LANES : 5 * LANES]

    cut = (whole // 2 + 7) // 8 * 8
    top, bottom = pl.ds(0, cut), pl.ds(cut, whole - cut)

    def reduce_start(p):
        r, s = p // 2, p % 2
        for t in range(tiles_j):
            value = planes_in[t, s * rows : (s + 1) * rows, :]
            high = value.astype(bf16)
            grid_hi[:, t * LANES : (t + 1) * LANES] = high
            grid_lo[:, t * LANES : (t + 1) * LANES] = (value - high.astype(f32)).astype(bf16)
        send = sum_send.at[p]
        analysis(p, far // 2)
        remote(
            partial.at[p, far, top], sum_a.at[p], send, sum_recv.at[p, 0], w, right
        ).start()
        remote(
            partial.at[p, far, bottom], sum_b.at[p], send, sum_recv.at[p, 1], w, left
        ).start()
        analysis(p, x // 2)
        remote(
            partial.at[p, right, bottom],
            sum_left.at[p, bottom],
            send,
            sum_recv.at[p, 2],
            w,
            right,
        ).start()
        remote(
            partial.at[p, left, top],
            sum_right.at[p, top],
            send,
            sum_recv.at[p, 3],
            w,
            left,
        ).start()

    def reduce_forward(p):
        send = sum_send.at[p]
        drain(sum_a.at[p], sum_recv.at[p, 0])
        partial[p, right, top, :] += sum_a[p]
        remote(
            partial.at[p, right, top],
            sum_left.at[p, top],
            send,
            sum_recv.at[p, 4],
            w,
            right,
        ).start()
        drain(sum_b.at[p], sum_recv.at[p, 1])
        partial[p, left, bottom, :] += sum_b[p]
        remote(
            partial.at[p, left, bottom],
            sum_right.at[p, bottom],
            send,
            sum_recv.at[p, 5],
            w,
            left,
        ).start()

    def solve(p):
        s = p % 2
        drain(sum_left.at[p, bottom], sum_recv.at[p, 2])
        drain(sum_right.at[p, top], sum_recv.at[p, 3])
        drain(sum_left.at[p, top], sum_recv.at[p, 4])
        drain(sum_right.at[p, bottom], sum_recv.at[p, 5])
        value = partial[p, x] + (sum_left[p] + sum_right[p])
        lanes = lax.broadcasted_iota(jnp.int32, (1, LANES), 1)
        start, odd = (x // 2) * half_n, x % 2
        first = start + odd * (half_n - 2 * LANES) + lanes
        middle = start + 2 * LANES + odd * half + lanes % half
        n = jnp.concatenate([first, first + LANES, middle], axis=1)
        mixed_part = value[2 * rows :]
        value = jnp.concatenate(
            [
                value[:rows],
                value[rows : 2 * rows],
                jnp.concatenate([mixed_part, pltpu.roll(mixed_part, half, 1)], axis=0),
            ],
            axis=1,
        )
        value = jnp.where(n >= zonal[2 * w + s], value, 0.0)
        factor = (n * (n + 1)).astype(f32) * (4.0 / (total * (total + 1)))
        both = jnp.dot(modal_in[...], value, precision=highest, preferred_element_type=f32)
        diagonal = lax.broadcasted_iota(jnp.int32, (size, size), 0) == lax.broadcasted_iota(
            jnp.int32, (size, size), 1
        )
        depth = jnp.sum(jnp.where(diagonal, eigen[...], 0.0), axis=1, keepdims=True)
        modal = (both[:size] + factor * both[size:]) / (1.0 + depth * factor)
        answer = jnp.dot(modal_out[...], modal, precision=highest, preferred_element_type=f32)
        thermal = lax.broadcasted_iota(jnp.int32, (rows, 1), 0) >= size
        answer = answer + jnp.where(thermal, value, 0.0)
        solved[p, x, 0:rows, :] = answer[:, :LANES]
        solved[p, x, rows : 2 * rows, :] = answer[:, LANES : 2 * LANES]
        last = answer[:, 2 * LANES :]
        low = lax.broadcasted_iota(jnp.int32, (size, LANES), 1) < half
        solved[p, x, 2 * rows :, :] = jnp.where(
            low, last[:size], pltpu.roll(last[size:], half, 1)
        )

    def gather_start(p):
        send = gather_send.at[p]
        for step in range(2):
            for to, first in ((right, 0), (left, 1)):
                part = (first, 1 - first)[step]
                at = (top, bottom)[part]
                remote(
                    solved.at[p, x, at],
                    solved.at[p, x, at],
                    send,
                    gather_recv.at[p, 2 * first + part],
                    w,
                    to,
                ).start()

    def gather_forward(p):
        send = gather_send.at[p]
        drain(solved.at[p, left, top], gather_recv.at[p, 0])
        remote(
            solved.at[p, left, top],
            solved.at[p, left, top],
            send,
            gather_recv.at[p, 4],
            w,
            right,
        ).start()
        drain(solved.at[p, right, bottom], gather_recv.at[p, 3])
        remote(
            solved.at[p, right, bottom],
            solved.at[p, right, bottom],
            send,
            gather_recv.at[p, 5],
            w,
            left,
        ).start()

    def gather_wait(p):
        drain(solved.at[p, left, bottom], gather_recv.at[p, 1])
        drain(solved.at[p, right, top], gather_recv.at[p, 2])
        drain(solved.at[p, far, top], gather_recv.at[p, 4])
        drain(solved.at[p, far, bottom], gather_recv.at[p, 5])

    def synthesis(p):
        s = p % 2
        low = lax.broadcasted_iota(jnp.int32, (size, LANES), 1) < half
        for h in range(2):
            even, odd, t = 2 * h, 2 * h + 1, h * (tiles_n // 2)
            mixed[t] = solved[p, even, 0:rows, :]
            mixed[t + 1] = solved[p, even, rows : 2 * rows, :]
            before, after = solved[p, even, 2 * rows :, :], solved[p, odd, 2 * rows :, :]
            mixed[t + 2, 0:size, :] = jnp.where(low, before, pltpu.roll(after, half, 1))
            mixed[t + 2, size:, :] = jnp.where(low, pltpu.roll(before, half, 1), after)
            mixed[t + 3] = solved[p, odd, 0:rows, :]
            mixed[t + 4] = solved[p, odd, rows : 2 * rows, :]
        for t in range(tiles_n):
            value = mixed[t]
            high = value.astype(bf16)
            spec_hi[:, t * LANES : (t + 1) * LANES] = high
            spec_lo[:, t * LANES : (t + 1) * LANES] = (value - high.astype(f32)).astype(bf16)
        start = 0
        while start < quarter:
            width = min(256, quarter - start)
            b_hi = leg_hi[s, :, start : start + width]
            b_lo = leg_lo[s, :, start : start + width]
            dot = functools.partial(jnp.dot, preferred_element_type=f32)
            value = dot(spec_hi[...], b_hi) + (
                dot(spec_hi[...], b_lo) + dot(spec_lo[...], b_hi)
            )
            for t in range(width // LANES):
                planes_out[start // LANES + t, s * rows : (s + 1) * rows, :] = value[
                    :, t * LANES : (t + 1) * LANES
                ]
            start += width

    def write_spectral(p):
        r, s = p // 2, p % 2
        for t in range(tiles_n):
            for i in range(per):
                for c in range(2):
                    for third in range(thirds):
                        spec_rows[
                            s,
                            per * third + i,
                            2 * c + r : 2 * c + r + 1,
                            t * LANES : (t + 1) * LANES,
                        ] = mixed[t, pl.ds(c * size + third * cells + x * per + i, 1), :]

    def pack(r, c):
        chunk = chunks[1][r][c]
        first, n = chunk
        lane = lax.broadcasted_iota(jnp.int32, (n, LANES), 1)

        @pl.loop(0, nx)
        def _(lg):
            tiles = [
                [
                    planes_out[t, pl.ds(first * cells + lg * per + i, n, stride=cells), :]
                    for t in range(tiles_j)
                ]
                for i in range(per)
            ]
            for b in range(near):
                value = None
                for i in range(per):
                    t, low = (b * band) // LANES, (b * band) % LANES
                    turn = (i * band - low) % LANES
                    moved = tiles[i][t]
                    moved = pltpu.roll(moved, turn, 1) if turn else moved
                    if low + band > LANES:
                        other = tiles[i][t + 1]
                        other = pltpu.roll(other, turn, 1) if turn else other
                        moved = jnp.where(lane >= i * band + LANES - low, other, moved)
                    value = moved if value is None else jnp.where(lane >= i * band, moved, value)
                packed[r, from_wave(lg * near + b, chunk), :] = value

    def collect(r):
        present = mask_present[...] > 0.5
        for k in range(pairs):
            for s in range(2):
                at = s * pairs + k
                first, n = next(chunk for chunk in chunks[1][r] if at < sum(chunk))
                square[k % 2, pl.ds(s, nw, stride=2), :] = final[
                    r, pl.ds(nw * first + at - first, nw, stride=n), :
                ]
            block = square[k % 2].T[: per * band].reshape(per, band, LANES)
            block = jnp.where(present[None], block, 0.0).reshape(per * band, LANES)
            result[pl.ds(first_row(r, k), per * band), :] = block

    def write_back(r):
        for c in range(2):
            at = pl.ds((2 * c + r) * lev * band, lev * band)
            pltpu.make_async_copy(
                result.at[at, :], fourier_new.at[at, :], out_sem.at[r, c]
            ).start()

    def write_back_wait(r):
        for c in range(2):
            at = pl.ds((2 * c + r) * lev * band, lev * band)
            pltpu.make_async_copy(
                result.at[at, :], fourier_new.at[at, :], out_sem.at[r, c]
            ).wait()

    def split(s):
        leg_copies[s].wait()
        chunk = 64

        @pl.loop(0, total // chunk)
        def _(k):
            at = pl.ds(pl.multiple_of(k * chunk, chunk), chunk)
            value = leg_full[s, at, :]
            high = value.astype(bf16)
            leg_hi[s, at, :] = high
            leg_lo[s, at, :] = (value - high.astype(f32)).astype(bf16)

    def matrices():
        exact = functools.partial(jnp.dot, precision=highest, preferred_element_type=f32)
        modal_in[:size, :] = exact(project[...], pick_div[...])
        modal_in[size:, :] = exact(exact(project[...], balance[...]), pick_temp[...])
        modal_out[...] = exact(place_div[...], modes[...]) - exact(
            place_temp[...], exact(reply[...], modes[...])
        )

    spread(0)
    pl.semaphore_wait(barrier, nw - 1 + nx - 1)
    wave_in(0, 1)
    wave_in(0, 0)
    spread(1)
    wave_in(0, 2)
    wave_in_wait(0, 1)
    lev_start(0, 0, 1)
    lev_wait(0, 0, 1)
    split(0)
    unpack(0, 1)
    matrices()
    wave_in_wait(0, 0)
    lev_start(0, 0, 0)
    wave_in(1, 0)
    wave_in_wait(0, 2)
    lev_start(0, 0, 2)
    lev_wait(0, 0, 0)
    unpack(0, 0)
    reduce_start(0)
    wave_in(1, 1)
    lev_wait(0, 0, 2)
    wave_in_wait(1, 0)
    lev_start(0, 1, 0)
    reduce_forward(0)
    split(1)
    wave_in(1, 2)
    unpack(0, 2)
    reduce_start(1)
    solve(0)
    wave_in_wait(1, 1)
    gather_start(0)
    reduce_forward(1)
    lev_start(0, 1, 1)
    gather_forward(0)
    wave_in_wait(1, 2)
    solve(1)
    lev_wait(0, 1, 0)
    lev_start(0, 1, 2)
    gather_start(1)
    gather_wait(0)
    lev_wait(0, 1, 1)
    synthesis(0)
    unpack(1, 0)
    unpack(1, 1)
    reduce_start(2)
    write_spectral(0)
    gather_forward(1)
    pack(0, 0)
    lev_wait(0, 1, 2)
    reduce_forward(2)
    unpack(1, 2)
    lev_start(1, 0, 0)
    gather_wait(1)
    reduce_start(3)
    synthesis(1)
    solve(2)
    pack(0, 2)
    lev_start(1, 0, 2)
    pack(0, 1)
    lev_wait(1, 0, 0)
    reduce_forward(3)
    gather_start(2)
    lev_wait(1, 0, 2)
    lev_start(1, 0, 1)
    wave_out(0, 0)
    gather_forward(2)
    solve(3)
    gather_start(3)
    wave_out(0, 2)
    lev_wait(1, 0, 1)
    wave_out(0, 1)
    gather_wait(2)
    write_spectral(1)
    synthesis(2)
    gather_forward(3)
    pack(1, 0)
    write_spectral(2)
    lev_start(1, 1, 0)
    gather_wait(3)
    wave_out_wait(0, 2)
    synthesis(3)
    write_spectral(3)
    pack(1, 1)
    lev_start(1, 1, 1)
    wave_out_wait(0, 0)
    lev_wait(1, 1, 0)
    wave_out(1, 0)
    pack(1, 2)
    lev_wait(1, 1, 1)
    wave_out_wait(0, 1)
    lev_start(1, 1, 2)
    collect(0)
    spec_copy = pltpu.make_async_copy(spec_rows, spectral, out_sem.at[0, 2])
    spec_copy.start()
    wave_out(1, 1)
    lev_wait(1, 1, 2)
    write_back(0)
    wave_out(1, 2)

    for kind in range(2):
        for r in range(2):
            for c, chunk in enumerate(chunks[kind][r]):
                drain(in_rows.at[r, all_waves(chunk, nw - 1), :], wave_send.at[kind, r, c])
                sent = nw - near
                drain(in_rows.at[r, all_waves(chunk, sent), :], lev_send.at[kind, r, c])
    for p in range(4):
        drain(solved.at[p, pl.ds(0, 3)], sum_send.at[p])
        drain(solved.at[p, pl.ds(0, 3)], gather_send.at[p])
    for c in range(len(chunks[1][1])):
        wave_out_wait(1, c)
    collect(1)
    write_back(1)
    spec_copy.wait()
    write_back_wait(0)
    write_back_wait(1)


def on_device(
    nw,
    nx,
    fourier,
    legendre,
    weights,
    points,
    zonal,
    pressure_balance_matrix,
    modes,
    project,
    eigen,
    thermal_reply_matrix,
):
    waves, parts, lev, band = fourier.shape
    slots, total, quarter = legendre.shape
    size = nx * lev
    per = LANES // band
    groups = parts * lev // per
    rows = 2 * size
    whole = 2 * rows + size
    cut = (whole // 2 + 7) // 8 * 8
    tiles_n = total // LANES
    dims = (nw, nx, band, lev, total, quarter)

    pick = np.zeros((2, size, rows), np.float32)
    row = 0
    for c in range(2):
        for third in range(lev // per):
            for group in range(nx):
                for i in range(per):
                    pick[c, group * lev + per * third + i, row] = 1.0
                    row += 1

    view = fourier.transpose(1, 2, 3, 0).reshape(parts * lev * band, waves)
    f32, bf16 = jnp.float32, jnp.bfloat16
    vmem = pl.BlockSpec(memory_space=pltpu.VMEM)
    smem = pl.BlockSpec(memory_space=pltpu.SMEM)
    anywhere = pl.BlockSpec(memory_space=pl.ANY)
    dma = pltpu.SemaphoreType.DMA
    lines = pltpu.VMEM((2, nw * groups, LANES), f32)
    spectral, fourier_new = pl.pallas_call(
        functools.partial(kernel, dims),
        out_shape=(
            jax.ShapeDtypeStruct((slots, lev, parts, total), f32),
            jax.ShapeDtypeStruct(view.shape, f32),
        ),
        in_specs=[vmem, anywhere, smem, smem, smem] + [vmem] * 10,
        out_specs=(anywhere, anywhere),
        scratch_shapes=[
            pltpu.VMEM((slots, total, quarter), f32),
            pltpu.VMEM((slots, total, quarter), bf16),
            pltpu.VMEM((slots, total, quarter), bf16),
            pltpu.VMEM((band, LANES), f32),
            pltpu.VMEM((band, LANES), f32),
            pltpu.VMEM((2, LANES, LANES), f32),
            lines,
            lines,
            lines,
            pltpu.VMEM((quarter // LANES, 2 * rows, LANES), f32),
            pltpu.VMEM((quarter // LANES, 2 * rows, LANES), f32),
            pltpu.VMEM((rows, quarter), bf16),
            pltpu.VMEM((rows, quarter), bf16),
            pltpu.VMEM((4, nx, whole, LANES), f32),
            pltpu.VMEM((4, cut, LANES), f32),
            pltpu.VMEM((4, whole - cut, LANES), f32),
            pltpu.VMEM((4, whole, LANES), f32),
            pltpu.VMEM((4, whole, LANES), f32),
            pltpu.VMEM((rows, rows), f32),
            pltpu.VMEM((rows, size), f32),
            pltpu.VMEM((4, nx, whole, LANES), f32),
            pltpu.VMEM((tiles_n, rows, LANES), f32),
            pltpu.VMEM((rows, total), bf16),
            pltpu.VMEM((rows, total), bf16),
            pltpu.VMEM((slots, lev, parts, total), f32),
            lines,
            lines,
            lines,
            pltpu.VMEM(view.shape, f32),
            dma((2,)),
            dma((2, 2, 3)),
            dma((2, 2, 3)),
            dma((2, 2, 3)),
            dma((2, 2, 3)),
            dma((4,)),
            dma((4, 6)),
            dma((4,)),
            dma((4, 6)),
            dma((2, 3)),
        ],
        compiler_params=pltpu.CompilerParams(
            collective_id=0, has_side_effects=True, vmem_limit_bytes=58 * 1024 * 1024
        ),
    )(
        view,
        legendre,
        weights,
        points,
        zonal,
        zonal.reshape(1, waves),
        pressure_balance_matrix,
        modes,
        project,
        eigen.reshape(1, size),
        thermal_reply_matrix,
        jnp.asarray(pick[0]),
        jnp.asarray(pick[1]),
        jnp.asarray(pick[0].T),
        jnp.asarray(pick[1].T),
    )
    spectral = spectral.transpose(0, 2, 1, 3)
    fourier_new = fourier_new.reshape(parts, lev, band, waves).transpose(3, 0, 1, 2)
    return (spectral, fourier_new)


def solution(mesh):
    return jax.shard_map(
        functools.partial(on_device, mesh.shape["wave"], mesh.shape["lev"]),
        mesh=mesh,
        in_specs=(
            P(None, None, "lev", "wave"),
            P("wave", None, "lev"),
            P(),
            P(),
            P(),
            P(),
            P(),
            P(),
            P(),
            P(),
        ),
        out_specs=(P("wave", None, "lev", None), P(None, None, "lev", "wave")),
        check_vma=False,
    )
```

```python
import functools

import jax
import jax.numpy as jnp
import numpy as np
from jax import lax
from jax.experimental import pallas as pl
from jax.experimental.pallas import tpu as pltpu
from jax.sharding import PartitionSpec as P

MESH = pl.DeviceIdType.MESH
LANES = 128
CHUNKS_IN = (((0, 8), (8, 8), (16, 8)), ((0, 8), (8, 8), (16, 8)))
WHOLE, LONG_FIRST, SHORT_FIRST = ((0, 12),), ((0, 8), (8, 4)), ((0, 4), (4, 8))
PARTS_SUM = (LONG_FIRST, WHOLE, WHOLE, WHOLE)
PARTS_GATHER = (WHOLE, WHOLE, WHOLE, SHORT_FIRST)
CHUNKS_OUT = (((0, 8), (8, 8), (16, 8)), ((0, 8), (8, 8), (16, 8)))


def kernel(
    dims,
    fourier,
    legendre,
    weights_far,
    points_far,
    zonal_far,
    balance_far,
    modes_far,
    project_far,
    eigen_far,
    reply_far,
    pick_div_far,
    pick_temp_far,
    place_div_far,
    place_temp_far,
    spectral,
    fourier_new,
    weights,
    points,
    zonal,
    balance,
    modes,
    project,
    eigen,
    reply,
    pick_div,
    pick_temp,
    place_div,
    place_temp,
    field,
    leg_full,
    leg_hi,
    leg_lo,
    mask_weight,
    mask_present,
    square,
    out_rows,
    in_rows,
    blocks,
    planes_in,
    planes_out,
    grid_hi,
    grid_lo,
    partial,
    sum_a,
    sum_b,
    sum_left,
    sum_right,
    modal_in,
    modal_out,
    solved,
    mixed,
    spec_hi,
    spec_lo,
    spec_rows,
    packed,
    returned,
    final,
    result,
    small_sem,
    field_sem,
    leg_sem,
    wave_send,
    wave_recv,
    lev_send,
    lev_recv,
    sum_send,
    sum_recv,
    gather_send,
    gather_recv,
    out_sem,
):
    nw, nx, band, lev, total, quarter = dims
    per = LANES // band
    thirds = lev // per
    pairs = 2 * thirds
    cells = nx * per
    groups = 2 * pairs
    near = nw // nx
    size = nx * lev
    rows = 2 * size
    tiles_j = quarter // LANES
    tiles_n = total // LANES
    half_n = total // 2
    half = LANES // 2
    whole = 2 * rows + size
    highest = lax.Precision.HIGHEST
    f32, bf16 = jnp.float32, jnp.bfloat16
    w = lax.axis_index("wave")
    x = lax.axis_index("lev")
    right, left, far = lax.rem(x + 1, nx), lax.rem(x + nx - 1, nx), lax.rem(x + 2, nx)
    chunks = (CHUNKS_IN, CHUNKS_OUT)

    def remote(src, dst, send, recv, to_w, to_x):
        return pltpu.make_async_remote_copy(
            src_ref=src,
            dst_ref=dst,
            send_sem=send,
            recv_sem=recv,
            device_id=(to_w, to_x),
            device_id_type=MESH,
        )

    def drain(ref, sem):
        pltpu.make_async_copy(ref, ref, sem).wait()

    barrier = pltpu.get_barrier_semaphore()

    @pl.loop(1, nw)
    def _(k):
        pl.semaphore_signal(
            barrier, inc=1, device_id=(lax.rem(w + k, nw), x), device_id_type=MESH
        )

    for k in range(1, nx):
        pl.semaphore_signal(
            barrier, inc=1, device_id=(w, lax.rem(x + k, nx)), device_id_type=MESH
        )

    def field_copies(r):
        parts = [pl.ds((2 * c + r) * lev * band, lev * band) for c in range(2)]
        return [
            pltpu.make_async_copy(fourier.at[at, :], field.at[at, :], field_sem.at[r, c])
            for c, at in enumerate(parts)
        ]

    for r in range(2):
        for copy in field_copies(r):
            copy.start()

    small_copies = [
        pltpu.make_async_copy(source, target, small_sem.at[i])
        for i, (source, target) in enumerate(
            (
                (weights_far, weights),
                (points_far, points),
                (zonal_far, zonal),
                (balance_far, balance),
                (modes_far, modes),
                (project_far, project),
                (eigen_far, eigen),
                (reply_far, reply),
                (pick_div_far, pick_div),
                (pick_temp_far, pick_temp),
                (place_div_far, place_div),
                (place_temp_far, place_temp),
            )
        )
    ]
    for copy in small_copies:
        copy.start()
    leg_copies = [
        pltpu.make_async_copy(legendre.at[s], leg_full.at[s], leg_sem.at[s])
        for s in range(2)
    ]
    for copy in leg_copies:
        copy.start()

    def own_zonal(s):
        places = lax.broadcasted_iota(jnp.int32, zonal.shape, 1)
        return jnp.sum(
            jnp.where(places == 2 * w + s, zonal[...], 0), axis=1, keepdims=True
        )

    def masks():
        for s in range(2):
            for t in range(tiles_j):
                at = pl.ds(x * tiles_j + t, 1)
                here = 2 * own_zonal(s) < points[at, :]
                row = slice(s * tiles_j + t, s * tiles_j + t + 1)
                mask_weight[row, :] = jnp.where(here, weights[at, :], 0.0)
                mask_present[row, :] = jnp.where(here, 1.0, 0.0)

    def first_row(r, k):
        c, third = k // thirds, k % thirds
        return pl.multiple_of(((2 * c + r) * lev + per * third) * band, 8)

    def spread(r, low, high):
        if low == 0:
            for copy in field_copies(r):
                copy.wait()

        @pl.loop(low, high)
        def _(k):
            block = field[pl.ds(first_row(r, k), per * band), :]
            block = jnp.concatenate(
                [block, jnp.zeros((LANES - per * band, LANES), f32)], axis=0
            )
            out_rows[r, pl.ds(k, 2 * nw, stride=pairs), :] = block.T

    def from_wave(index, chunk):
        first, n = chunk
        return pl.ds(pl.multiple_of(nw * first + index * n, 8), n)

    def all_waves(chunk, count=nw):
        first, n = chunk
        return pl.ds(nw * first, count * n)

    def wave_exchange(kind, r, c, source, target):
        send, recv = wave_send.at[kind, r, c], wave_recv.at[kind, r, c]

        @pl.loop(1, nw)
        def _(k):
            to = lax.rem(w + k, nw)
            remote(source(to), target, send, recv, to, x).start()

        pltpu.make_async_copy(source(w), target, recv).start()

    def wave_in(r, c):
        chunk = chunks[0][r][c]
        first, n = chunk
        wave_exchange(
            0,
            r,
            c,
            lambda to: out_rows.at[r, pl.ds(pl.multiple_of(to * groups + first, 8), n), :],
            in_rows.at[r, from_wave(w, chunk), :],
        )

    def wave_in_wait(r, c):
        drain(in_rows.at[r, all_waves(chunks[0][r][c]), :], wave_recv.at[0, r, c])

    def wave_out(r, c):
        chunk = chunks[1][r][c]
        wave_exchange(
            1,
            r,
            c,
            lambda to: returned.at[r, from_wave(to, chunk), :],
            final.at[r, from_wave(w, chunk), :],
        )

    def wave_out_wait(r, c):
        drain(final.at[r, all_waves(chunks[1][r][c]), :], wave_recv.at[1, r, c])

    def span(q, chunk):
        first, n = chunk
        return pl.ds(pl.multiple_of(nw * first + q * (near * n), 8), near * n)

    def lev_start(kind, r, c):
        source, target = ((in_rows, blocks), (packed, returned))[kind]
        chunk = chunks[kind][r][c]
        send, recv = lev_send.at[kind, r, c], lev_recv.at[kind, r, c]
        for to in (far, right, left):
            remote(
                source.at[r, span(to, chunk), :],
                target.at[r, span(x, chunk), :],
                send,
                recv,
                w,
                to,
            ).start()
        pltpu.make_async_copy(
            source.at[r, span(x, chunk), :], target.at[r, span(x, chunk), :], recv
        ).start()

    def lev_wait(kind, r, c):
        target = (blocks, returned)[kind]
        drain(target.at[r, all_waves(chunks[kind][r][c]), :], lev_recv.at[kind, r, c])

    def unpack(r, c):
        chunk = chunks[0][r][c]
        first, n = chunk
        lane = lax.broadcasted_iota(jnp.int32, (n, LANES), 1)

        @pl.loop(0, nx)
        def _(lg):
            bands = [
                blocks[r, from_wave(lg * near + b, chunk), :]
                for b in range(near)
            ]
            for i in range(per):
                at = pl.ds(first * cells + lg * per + i, n, stride=cells)
                for t in range(tiles_j):
                    value = None
                    for b in range(near):
                        low = b * band - t * LANES
                        if low + band <= 0 or low >= LANES:
                            continue
                        turn = (low - i * band) % LANES
                        moved = pltpu.roll(bands[b], turn, 1) if turn else bands[b]
                        value = moved if value is None else jnp.where(lane >= low, moved, value)
                    planes_in[t, at, :] = value

    def places(parts, u):
        before = [0, 0]
        for v, (first, count) in enumerate(parts):
            start, m = first * cells, count * cells
            offset, length = start * 5 // 2, m * 5 // 2
            cut = (length // 2 + 7) // 8 * 8
            if v == u:
                return (
                    (start, m, offset),
                    pl.ds(offset, cut),
                    pl.ds(offset + cut, length - cut),
                    pl.ds(before[0], cut),
                    pl.ds(before[1], length - cut),
                )
            before = [before[0] + cut, before[1] + length - cut]

    def analysis(p, u, h):
        s = p % 2
        start, m, offset = places(PARTS_SUM[p], u)[0]
        n_at = pl.ds(pl.multiple_of(h * half_n, 16), half_n)
        a_hi, a_lo = grid_hi[start : start + m, :], grid_lo[start : start + m, :]
        b_hi, b_lo = leg_hi[s, n_at, :], leg_lo[s, n_at, :]
        dot = functools.partial(
            lax.dot_general,
            dimension_numbers=(((1,), (1,)), ((), ())),
            preferred_element_type=f32,
        )
        value = dot(a_hi, b_hi) + (dot(a_hi, b_lo) + dot(a_lo, b_hi))
        low = lax.broadcasted_iota(jnp.int32, (m // 2, LANES), 1) < half
        even, odd = 2 * h, 2 * h + 1
        one, two, three = (pl.ds(offset, m), pl.ds(offset + m, m), pl.ds(offset + 2 * m, m // 2))
        partial[p, even, one, :] = value[:, 0:LANES]
        partial[p, even, two, :] = value[:, LANES : 2 * LANES]
        middle = value[:, 2 * LANES : 3 * LANES]
        first, second = middle[: m // 2], middle[m // 2 :]
        partial[p, even, three, :] = jnp.where(low, first, pltpu.roll(second, half, 1))
        partial[p, odd, three, :] = jnp.where(low, pltpu.roll(first, half, 1), second)
        partial[p, odd, one, :] = value[:, 3 * LANES : 4 * LANES]
        partial[p, odd, two, :] = value[:, 4 * LANES : 5 * LANES]

    def reduce_start(p, u):
        s = p % 2
        (start, m, _), top, bottom, at_a, at_b = places(PARTS_SUM[p], u)
        for t in range(tiles_j):
            value = planes_in[t, s * rows + start : s * rows + start + m, :]
            value = value * mask_weight[s * tiles_j + t : s * tiles_j + t + 1, :]
            high = value.astype(bf16)
            lanes = slice(t * LANES, (t + 1) * LANES)
            grid_hi[start : start + m, lanes] = high
            grid_lo[start : start + m, lanes] = (value - high.astype(f32)).astype(bf16)
        send, recv = sum_send.at[p], sum_recv.at[p, u]
        analysis(p, u, far // 2)
        remote(partial.at[p, far, top], sum_a.at[p, at_a], send, recv.at[0], w, right).start()
        remote(partial.at[p, far, bottom], sum_b.at[p, at_b], send, recv.at[1], w, left).start()
        analysis(p, u, x // 2)
        remote(
            partial.at[p, right, bottom], sum_left.at[p, bottom], send, recv.at[2], w, right
        ).start()
        remote(partial.at[p, left, top], sum_right.at[p, top], send, recv.at[3], w, left).start()

    def reduce_forward(p, u):
        _, top, bottom, at_a, at_b = places(PARTS_SUM[p], u)
        send, recv = sum_send.at[p], sum_recv.at[p, u]
        drain(sum_a.at[p, at_a], recv.at[0])
        partial[p, right, top, :] += sum_a[p, at_a, :]
        remote(partial.at[p, right, top], sum_left.at[p, top], send, recv.at[4], w, right).start()
        drain(sum_b.at[p, at_b], recv.at[1])
        partial[p, left, bottom, :] += sum_b[p, at_b, :]
        remote(
            partial.at[p, left, bottom], sum_right.at[p, bottom], send, recv.at[5], w, left
        ).start()

    def solve(p):
        s = p % 2
        pieces = []
        for u in range(len(PARTS_SUM[p])):
            (_, m, offset), top, bottom, _, _ = places(PARTS_SUM[p], u)
            recv = sum_recv.at[p, u]
            drain(sum_left.at[p, bottom], recv.at[2])
            drain(sum_right.at[p, top], recv.at[3])
            drain(sum_left.at[p, top], recv.at[4])
            drain(sum_right.at[p, bottom], recv.at[5])
            at = pl.ds(offset, m * 5 // 2)
            value = partial[p, x, at, :] + (sum_left[p, at, :] + sum_right[p, at, :])
            last = value[2 * m :]
            pieces.append(
                jnp.concatenate(
                    [
                        value[:m],
                        value[m : 2 * m],
                        jnp.concatenate([last, pltpu.roll(last, half, 1)], axis=0),
                    ],
                    axis=1,
                )
            )
        value = pieces[0] if len(pieces) == 1 else jnp.concatenate(pieces, axis=0)
        lanes = lax.broadcasted_iota(jnp.int32, (1, LANES), 1)
        begin, odd = (x // 2) * half_n, x % 2
        first = begin + odd * (half_n - 2 * LANES) + lanes
        middle = begin + 2 * LANES + odd * half + lanes % half
        n = jnp.concatenate([first, first + LANES, middle], axis=1)
        value = jnp.where(n >= own_zonal(s), value, 0.0)
        factor = (n * (n + 1)).astype(f32) * (4.0 / (total * (total + 1)))
        both = jnp.dot(modal_in[...], value, precision=highest, preferred_element_type=f32)
        diagonal = lax.broadcasted_iota(jnp.int32, (size, size), 0) == lax.broadcasted_iota(
            jnp.int32, (size, size), 1
        )
        depth = jnp.sum(jnp.where(diagonal, eigen[...], 0.0), axis=1, keepdims=True)
        modal = (both[:size] + factor * both[size:]) / (1.0 + depth * factor)
        answer = jnp.dot(modal_out[...], modal, precision=highest, preferred_element_type=f32)
        thermal = lax.broadcasted_iota(jnp.int32, (rows, 1), 0) >= size
        answer = answer + jnp.where(thermal, value, 0.0)
        for u in range(len(PARTS_GATHER[p])):
            start, m, offset = places(PARTS_GATHER[p], u)[0]
            low = lax.broadcasted_iota(jnp.int32, (m // 2, LANES), 1) < half
            part = answer[start : start + m]
            solved[p, x, pl.ds(offset, m), :] = part[:, :LANES]
            solved[p, x, pl.ds(offset + m, m), :] = part[:, LANES : 2 * LANES]
            last = part[:, 2 * LANES :]
            solved[p, x, pl.ds(offset + 2 * m, m // 2), :] = jnp.where(
                low, last[: m // 2], pltpu.roll(last[m // 2 :], half, 1)
            )

    def gather_start(p):
        send = gather_send.at[p]
        for u in range(len(PARTS_GATHER[p])):
            halves = places(PARTS_GATHER[p], u)[1:3]
            for step in range(2):
                for to, first in ((right, 0), (left, 1)):
                    part = (first, 1 - first)[step]
                    block = solved.at[p, x, halves[part]]
                    remote(
                        block, block, send, gather_recv.at[p, u, 2 * first + part], w, to
                    ).start()

    def gather_forward(p, u):
        _, top, bottom, _, _ = places(PARTS_GATHER[p], u)
        send, recv = gather_send.at[p], gather_recv.at[p, u]
        for block, got, index, to in (
            (solved.at[p, left, top], 0, 4, right),
            (solved.at[p, right, bottom], 3, 5, left),
        ):
            drain(block, recv.at[got])
            remote(block, block, send, recv.at[index], w, to).start()

    def gather_wait(p, u):
        _, top, bottom, _, _ = places(PARTS_GATHER[p], u)
        recv = gather_recv.at[p, u]
        drain(solved.at[p, left, bottom], recv.at[1])
        drain(solved.at[p, right, top], recv.at[2])
        drain(solved.at[p, far, top], recv.at[4])
        drain(solved.at[p, far, bottom], recv.at[5])

    def synthesis(p, u):
        s = p % 2
        start, m, offset = places(PARTS_GATHER[p], u)[0]
        low = lax.broadcasted_iota(jnp.int32, (m // 2, LANES), 1) < half
        one, two, three = (pl.ds(offset, m), pl.ds(offset + m, m), pl.ds(offset + 2 * m, m // 2))
        at, upper, lower = (pl.ds(start, m), pl.ds(start, m // 2), pl.ds(start + m // 2, m // 2))
        for h in range(2):
            even, odd, t = 2 * h, 2 * h + 1, h * (tiles_n // 2)
            mixed[t, at, :] = solved[p, even, one, :]
            mixed[t + 1, at, :] = solved[p, even, two, :]
            before, after = solved[p, even, three, :], solved[p, odd, three, :]
            mixed[t + 2, upper, :] = jnp.where(low, before, pltpu.roll(after, half, 1))
            mixed[t + 2, lower, :] = jnp.where(low, pltpu.roll(before, half, 1), after)
            mixed[t + 3, at, :] = solved[p, odd, one, :]
            mixed[t + 4, at, :] = solved[p, odd, two, :]
        for t in range(tiles_n):
            value = mixed[t, at, :]
            high = value.astype(bf16)
            lanes = slice(t * LANES, (t + 1) * LANES)
            spec_hi[start : start + m, lanes] = high
            spec_lo[start : start + m, lanes] = (value - high.astype(f32)).astype(bf16)
        a_hi, a_lo = spec_hi[start : start + m, :], spec_lo[start : start + m, :]
        begin = 0
        while begin < quarter:
            width = min(256, quarter - begin)
            b_hi = leg_hi[s, :, begin : begin + width]
            b_lo = leg_lo[s, :, begin : begin + width]
            dot = functools.partial(jnp.dot, preferred_element_type=f32)
            value = dot(a_hi, b_hi) + (dot(a_hi, b_lo) + dot(a_lo, b_hi))
            for t in range(width // LANES):
                tile = begin // LANES + t
                row = s * tiles_j + tile
                here = mask_present[row : row + 1, :] > 0.5
                planes_out[tile, pl.ds(s * rows + start, m), :] = jnp.where(
                    here, value[:, t * LANES : (t + 1) * LANES], 0.0
                )
            begin += width

    def write_spectral(p, u):
        r, s = p // 2, p % 2
        first, count = PARTS_GATHER[p][u]
        for t in range(tiles_n):
            for i in range(per):
                for k in range(first, first + count):
                    c, third = k // thirds, k % thirds
                    spec_rows[
                        s,
                        per * third + i,
                        2 * c + r : 2 * c + r + 1,
                        t * LANES : (t + 1) * LANES,
                    ] = mixed[t, pl.ds(k * cells + x * per + i, 1), :]

    def pack(r, c):
        chunk = chunks[1][r][c]
        first, n = chunk
        lane = lax.broadcasted_iota(jnp.int32, (n, LANES), 1)

        @pl.loop(0, nx)
        def _(lg):
            tiles = [
                [
                    planes_out[t, pl.ds(first * cells + lg * per + i, n, stride=cells), :]
                    for t in range(tiles_j)
                ]
                for i in range(per)
            ]
            for b in range(near):
                value = None
                for i in range(per):
                    t, low = (b * band) // LANES, (b * band) % LANES
                    turn = (i * band - low) % LANES
                    moved = tiles[i][t]
                    moved = pltpu.roll(moved, turn, 1) if turn else moved
                    if low + band > LANES:
                        other = tiles[i][t + 1]
                        other = pltpu.roll(other, turn, 1) if turn else other
                        moved = jnp.where(lane >= i * band + LANES - low, other, moved)
                    value = moved if value is None else jnp.where(lane >= i * band, moved, value)
                packed[r, from_wave(lg * near + b, chunk), :] = value

    def write_back(r, c):
        at = pl.ds((2 * c + r) * lev * band, lev * band)
        return pltpu.make_async_copy(result.at[at, :], fourier_new.at[at, :], out_sem.at[r, c])

    def collect(r):
        for k in range(pairs):
            for s in range(2):
                at = s * pairs + k
                first, n = next(chunk for chunk in chunks[1][r] if at < sum(chunk))
                square[k % 2, pl.ds(s, nw, stride=2), :] = final[
                    r, pl.ds(nw * first + at - first, nw, stride=n), :
                ]
            result[pl.ds(first_row(r, k), per * band), :] = square[k % 2].T[: per * band]
            if k % thirds == thirds - 1:
                write_back(r, k // thirds).start()

    def split(s):
        leg_copies[s].wait()
        chunk = 64

        @pl.loop(0, total // chunk)
        def _(k):
            at = pl.ds(pl.multiple_of(k * chunk, chunk), chunk)
            value = leg_full[s, at, :]
            high = value.astype(bf16)
            leg_hi[s, at, :] = high
            leg_lo[s, at, :] = (value - high.astype(f32)).astype(bf16)

    def matrices():
        for copy in small_copies:
            copy.wait()
        masks()
        exact = functools.partial(jnp.dot, precision=highest, preferred_element_type=f32)
        modal_in[:size, :] = exact(project[...], pick_div[...])
        modal_in[size:, :] = exact(exact(project[...], balance[...]), pick_temp[...])
        modal_out[...] = exact(place_div[...], modes[...]) - exact(
            place_temp[...], exact(reply[...], modes[...])
        )

    spread(0, 0, chunks[0][0][0][1])
    pl.semaphore_wait(barrier, nw - 1 + nx - 1)
    wave_in(0, 0)
    spread(0, chunks[0][0][0][1], pairs)
    split(0)
    wave_in(0, 1)
    wave_in(0, 2)
    matrices()
    wave_in_wait(0, 0)
    spread(1, 0, pairs)
    lev_start(0, 0, 0)
    wave_in_wait(0, 1)
    lev_start(0, 0, 1)
    wave_in(1, 1)
    wave_in(1, 0)
    lev_wait(0, 0, 0)
    unpack(0, 0)
    reduce_start(0, 0)
    lev_wait(0, 0, 1)
    unpack(0, 1)
    wave_in_wait(0, 2)
    lev_start(0, 0, 2)
    wave_in(1, 2)
    reduce_forward(0, 0)
    reduce_start(0, 1)
    split(1)
    wave_in_wait(1, 1)
    lev_start(0, 1, 1)
    lev_wait(0, 0, 2)
    unpack(0, 2)
    reduce_forward(0, 1)
    reduce_start(1, 0)
    solve(0)
    wave_in_wait(1, 0)
    gather_start(0)
    reduce_forward(1, 0)
    lev_start(0, 1, 0)
    lev_wait(0, 1, 1)
    gather_forward(0, 0)
    wave_in_wait(1, 2)
    unpack(1, 1)
    solve(1)
    lev_start(0, 1, 2)
    gather_start(1)
    gather_wait(0, 0)
    lev_wait(0, 1, 0)
    synthesis(0, 0)
    unpack(1, 0)
    pack(0, 0)
    reduce_start(2, 0)
    gather_forward(1, 0)
    lev_start(1, 0, 0)
    write_spectral(0, 0)
    lev_wait(0, 1, 2)
    unpack(1, 2)
    reduce_start(3, 0)
    gather_wait(1, 0)
    reduce_forward(2, 0)
    lev_wait(1, 0, 0)
    synthesis(1, 0)
    pack(0, 1)
    lev_start(1, 0, 1)
    reduce_forward(3, 0)
    write_spectral(1, 0)
    wave_out(0, 0)
    solve(2)
    pack(0, 2)
    gather_start(2)
    lev_wait(1, 0, 1)
    lev_start(1, 0, 2)
    gather_forward(2, 0)
    solve(3)
    wave_out(0, 1)
    gather_start(3)
    lev_wait(1, 0, 2)
    wave_out(0, 2)
    gather_wait(2, 0)
    synthesis(2, 0)
    gather_forward(3, 0)
    pack(1, 0)
    lev_start(1, 1, 0)
    write_spectral(2, 0)
    gather_wait(3, 0)
    synthesis(3, 0)
    wave_out_wait(0, 1)
    gather_forward(3, 1)
    pack(1, 1)
    lev_start(1, 1, 1)
    lev_wait(1, 1, 0)
    wave_out(1, 0)
    gather_wait(3, 1)
    wave_out_wait(0, 0)
    synthesis(3, 1)
    pack(1, 2)
    wave_out_wait(0, 2)
    lev_start(1, 1, 2)
    write_spectral(3, 0)
    write_spectral(3, 1)
    lev_wait(1, 1, 1)
    wave_out(1, 1)
    collect(0)
    lev_wait(1, 1, 2)
    spec_copy = pltpu.make_async_copy(spec_rows, spectral, out_sem.at[0, 2])
    spec_copy.start()
    wave_out(1, 2)

    for kind in range(2):
        for r in range(2):
            for c, chunk in enumerate(chunks[kind][r]):
                drain(in_rows.at[r, all_waves(chunk, nw - 1), :], wave_send.at[kind, r, c])
                sent = nw - near
                drain(in_rows.at[r, all_waves(chunk, sent), :], lev_send.at[kind, r, c])
    for p in range(4):
        drain(solved.at[p, pl.ds(0, 3)], sum_send.at[p])
        drain(solved.at[p, pl.ds(0, 3)], gather_send.at[p])
    for c in range(len(chunks[1][1])):
        wave_out_wait(1, c)
    collect(1)
    spec_copy.wait()
    for r in range(2):
        for c in range(2):
            write_back(r, c).wait()


def on_device(
    nw,
    nx,
    fourier,
    legendre,
    weights,
    points,
    zonal,
    pressure_balance_matrix,
    modes,
    project,
    eigen,
    thermal_reply_matrix,
):
    waves, parts, lev, band = fourier.shape
    slots, total, quarter = legendre.shape
    size = nx * lev
    per = LANES // band
    groups = parts * lev // per
    rows = 2 * size
    whole = 2 * rows + size
    cut = (whole // 2 + 7) // 8 * 8
    tiles_n = total // LANES
    dims = (nw, nx, band, lev, total, quarter)

    pick = np.zeros((2, size, rows), np.float32)
    row = 0
    for c in range(2):
        for third in range(lev // per):
            for group in range(nx):
                for i in range(per):
                    pick[c, group * lev + per * third + i, row] = 1.0
                    row += 1

    view = fourier.transpose(1, 2, 3, 0).reshape(parts * lev * band, waves)
    f32, bf16 = jnp.float32, jnp.bfloat16
    anywhere = pl.BlockSpec(memory_space=pl.ANY)
    dma = pltpu.SemaphoreType.DMA
    lines = pltpu.VMEM((2, nw * groups, LANES), f32)
    spectral, fourier_new = pl.pallas_call(
        functools.partial(kernel, dims),
        out_shape=(
            jax.ShapeDtypeStruct((slots, lev, parts, total), f32),
            jax.ShapeDtypeStruct(view.shape, f32),
        ),
        in_specs=[anywhere] * 14,
        out_specs=(anywhere, anywhere),
        scratch_shapes=[
            pltpu.VMEM((weights.shape[0] // LANES, LANES), f32),
            pltpu.VMEM((weights.shape[0] // LANES, LANES), jnp.int32),
            pltpu.VMEM((1, waves), jnp.int32),
            pltpu.VMEM((size, size), f32),
            pltpu.VMEM((size, size), f32),
            pltpu.VMEM((size, size), f32),
            pltpu.VMEM((1, size), f32),
            pltpu.VMEM((size, size), f32),
            pltpu.VMEM((size, rows), f32),
            pltpu.VMEM((size, rows), f32),
            pltpu.VMEM((rows, size), f32),
            pltpu.VMEM((rows, size), f32),
            pltpu.VMEM(view.shape, f32),
            pltpu.VMEM((slots, total, quarter), f32),
            pltpu.VMEM((slots, total, quarter), bf16),
            pltpu.VMEM((slots, total, quarter), bf16),
            pltpu.VMEM((2 * (quarter // LANES), LANES), f32),
            pltpu.VMEM((2 * (quarter // LANES), LANES), f32),
            pltpu.VMEM((2, LANES, LANES), f32),
            lines,
            lines,
            lines,
            pltpu.VMEM((quarter // LANES, 2 * rows, LANES), f32),
            pltpu.VMEM((quarter // LANES, 2 * rows, LANES), f32),
            pltpu.VMEM((rows, quarter), bf16),
            pltpu.VMEM((rows, quarter), bf16),
            pltpu.VMEM((4, nx, whole, LANES), f32),
            pltpu.VMEM((4, cut, LANES), f32),
            pltpu.VMEM((4, cut, LANES), f32),
            pltpu.VMEM((4, whole, LANES), f32),
            pltpu.VMEM((4, whole, LANES), f32),
            pltpu.VMEM((rows, rows), f32),
            pltpu.VMEM((rows, size), f32),
            pltpu.VMEM((4, nx, whole, LANES), f32),
            pltpu.VMEM((tiles_n, rows, LANES), f32),
            pltpu.VMEM((rows, total), bf16),
            pltpu.VMEM((rows, total), bf16),
            pltpu.VMEM((slots, lev, parts, total), f32),
            lines,
            lines,
            lines,
            pltpu.VMEM(view.shape, f32),
            dma((12,)),
            dma((2, 2)),
            dma((2,)),
            dma((2, 2, 3)),
            dma((2, 2, 3)),
            dma((2, 2, 3)),
            dma((2, 2, 3)),
            dma((4,)),
            dma((4, 2, 6)),
            dma((4,)),
            dma((4, 2, 6)),
            dma((2, 3)),
        ],
        compiler_params=pltpu.CompilerParams(
            collective_id=0, has_side_effects=True, vmem_limit_bytes=58 * 1024 * 1024
        ),
    )(
        view,
        legendre,
        weights.reshape(-1, LANES),
        points.reshape(-1, LANES),
        zonal.reshape(1, waves),
        pressure_balance_matrix,
        modes,
        project,
        eigen.reshape(1, size),
        thermal_reply_matrix,
        jnp.asarray(pick[0]),
        jnp.asarray(pick[1]),
        jnp.asarray(pick[0].T),
        jnp.asarray(pick[1].T),
    )
    spectral = spectral.transpose(0, 2, 1, 3)
    fourier_new = fourier_new.reshape(parts, lev, band, waves).transpose(3, 0, 1, 2)
    return (spectral, fourier_new)


def solution(mesh):
    return jax.shard_map(
        functools.partial(on_device, mesh.shape["wave"], mesh.shape["lev"]),
        mesh=mesh,
        in_specs=(
            P(None, None, "lev", "wave"),
            P("wave", None, "lev"),
            P(),
            P(),
            P(),
            P(),
            P(),
            P(),
            P(),
            P(),
        ),
        out_specs=(P("wave", None, "lev", None), P(None, None, "lev", "wave")),
        check_vma=False,
    )
```

```python
import functools

import jax
import jax.numpy as jnp
import numpy as np
from jax import lax
from jax.experimental import pallas as pl
from jax.experimental.pallas import tpu as pltpu
from jax.sharding import PartitionSpec as P

MESH = pl.DeviceIdType.MESH
LANES = 128
CHUNKS_IN = (((0, 8), (8, 8), (16, 8)), ((0, 8), (8, 8), (16, 8)))
WHOLE, LONG_FIRST, SHORT_FIRST = ((0, 12),), ((0, 8), (8, 4)), ((0, 4), (4, 8))
PARTS_SUM = (LONG_FIRST, WHOLE, WHOLE, WHOLE)
PARTS_GATHER = (WHOLE, WHOLE, WHOLE, SHORT_FIRST)
CHUNKS_OUT = (((0, 8), (8, 8), (16, 8)), ((0, 8), (8, 8), (16, 8)))


def kernel(
    dims,
    fourier,
    legendre,
    weights_far,
    points_far,
    zonal_far,
    balance_far,
    modes_far,
    project_far,
    eigen_far,
    reply_far,
    pick_div_far,
    pick_temp_far,
    place_div_far,
    place_temp_far,
    spectral,
    fourier_new,
    weights,
    points,
    zonal,
    balance,
    modes,
    project,
    eigen,
    reply,
    pick_div,
    pick_temp,
    place_div,
    place_temp,
    field,
    leg_full,
    leg_hi,
    leg_lo,
    mask_weight,
    mask_present,
    square,
    out_rows,
    in_rows,
    blocks,
    planes_in,
    planes_out,
    grid_hi,
    grid_lo,
    partial,
    sum_a,
    sum_b,
    sum_left,
    sum_right,
    modal_in,
    modal_out,
    solved,
    mixed,
    spec_hi,
    spec_lo,
    spec_rows,
    packed,
    returned,
    final,
    result,
    small_sem,
    field_sem,
    leg_sem,
    wave_send,
    wave_recv,
    lev_send,
    lev_recv,
    sum_send,
    sum_recv,
    gather_send,
    gather_recv,
    out_sem,
):
    nw, nx, band, lev, total, quarter = dims
    per = LANES // band
    thirds = lev // per
    pairs = 2 * thirds
    cells = nx * per
    groups = 2 * pairs
    near = nw // nx
    size = nx * lev
    rows = 2 * size
    tiles_j = quarter // LANES
    tiles_n = total // LANES
    half_n = total // 2
    half = LANES // 2
    whole = 2 * rows + size
    highest = lax.Precision.HIGHEST
    f32, bf16 = jnp.float32, jnp.bfloat16
    w = lax.axis_index("wave")
    x = lax.axis_index("lev")
    right, left, far = lax.rem(x + 1, nx), lax.rem(x + nx - 1, nx), lax.rem(x + 2, nx)
    chunks = (CHUNKS_IN, CHUNKS_OUT)

    def remote(src, dst, send, recv, to_w, to_x):
        return pltpu.make_async_remote_copy(
            src_ref=src,
            dst_ref=dst,
            send_sem=send,
            recv_sem=recv,
            device_id=(to_w, to_x),
            device_id_type=MESH,
        )

    def drain(ref, sem):
        pltpu.make_async_copy(ref, ref, sem).wait()

    barrier = pltpu.get_barrier_semaphore()

    @pl.loop(1, nw)
    def _(k):
        pl.semaphore_signal(
            barrier, inc=1, device_id=(lax.rem(w + k, nw), x), device_id_type=MESH
        )

    for k in range(1, nx):
        pl.semaphore_signal(
            barrier, inc=1, device_id=(w, lax.rem(x + k, nx)), device_id_type=MESH
        )

    def field_copies(r):
        parts = [pl.ds((2 * c + r) * lev * band, lev * band) for c in range(2)]
        return [
            pltpu.make_async_copy(fourier.at[at, :], field.at[at, :], field_sem.at[r, c])
            for c, at in enumerate(parts)
        ]

    for r in range(2):
        for copy in field_copies(r):
            copy.start()

    small_copies = [
        pltpu.make_async_copy(source, target, small_sem.at[i])
        for i, (source, target) in enumerate(
            (
                (weights_far, weights),
                (points_far, points),
                (zonal_far, zonal),
                (balance_far, balance),
                (modes_far, modes),
                (project_far, project),
                (eigen_far, eigen),
                (reply_far, reply),
                (pick_div_far, pick_div),
                (pick_temp_far, pick_temp),
                (place_div_far, place_div),
                (place_temp_far, place_temp),
            )
        )
    ]
    for copy in small_copies:
        copy.start()
    leg_copies = [
        pltpu.make_async_copy(legendre.at[s], leg_full.at[s], leg_sem.at[s])
        for s in range(2)
    ]
    for copy in leg_copies:
        copy.start()

    def own_zonal(s):
        places = lax.broadcasted_iota(jnp.int32, zonal.shape, 1)
        return jnp.sum(
            jnp.where(places == 2 * w + s, zonal[...], 0), axis=1, keepdims=True
        )

    def masks():
        for s in range(2):
            for t in range(tiles_j):
                at = pl.ds(x * tiles_j + t, 1)
                here = 2 * own_zonal(s) < points[at, :]
                row = slice(s * tiles_j + t, s * tiles_j + t + 1)
                mask_weight[row, :] = jnp.where(here, weights[at, :], 0.0)
                mask_present[row, :] = jnp.where(here, 1.0, 0.0)

    def first_row(r, k):
        c, third = k // thirds, k % thirds
        return pl.multiple_of(((2 * c + r) * lev + per * third) * band, 8)

    def spread(r, low, high):
        if low == 0:
            for copy in field_copies(r):
                copy.wait()

        @pl.loop(low, high)
        def _(k):
            block = field[pl.ds(first_row(r, k), per * band), :]
            block = jnp.concatenate(
                [block, jnp.zeros((LANES - per * band, LANES), f32)], axis=0
            )
            out_rows[r, pl.ds(k, 2 * nw, stride=pairs), :] = block.T

    def from_wave(index, chunk):
        first, n = chunk
        return pl.ds(pl.multiple_of(nw * first + index * n, 8), n)

    def all_waves(chunk, count=nw):
        first, n = chunk
        return pl.ds(nw * first, count * n)

    def wave_exchange(kind, r, c, source, target):
        send, recv = wave_send.at[kind, r, c], wave_recv.at[kind, r, c]

        @pl.loop(1, nw)
        def _(k):
            to = lax.rem(w + k, nw)
            remote(source(to), target, send, recv, to, x).start()

        pltpu.make_async_copy(source(w), target, recv).start()

    def wave_in(r, c):
        chunk = chunks[0][r][c]
        first, n = chunk
        wave_exchange(
            0,
            r,
            c,
            lambda to: out_rows.at[r, pl.ds(pl.multiple_of(to * groups + first, 8), n), :],
            in_rows.at[r, from_wave(w, chunk), :],
        )

    def wave_in_wait(r, c):
        drain(in_rows.at[r, all_waves(chunks[0][r][c]), :], wave_recv.at[0, r, c])

    def wave_out(r, c):
        chunk = chunks[1][r][c]
        wave_exchange(
            1,
            r,
            c,
            lambda to: returned.at[r, from_wave(to, chunk), :],
            final.at[r, from_wave(w, chunk), :],
        )

    def wave_out_wait(r, c):
        drain(final.at[r, all_waves(chunks[1][r][c]), :], wave_recv.at[1, r, c])

    def span(q, chunk):
        first, n = chunk
        return pl.ds(pl.multiple_of(nw * first + q * (near * n), 8), near * n)

    def lev_start(kind, r, c):
        source, target = ((in_rows, blocks), (packed, returned))[kind]
        chunk = chunks[kind][r][c]
        send, recv = lev_send.at[kind, r, c], lev_recv.at[kind, r, c]
        for to in (far, right, left):
            remote(
                source.at[r, span(to, chunk), :],
                target.at[r, span(x, chunk), :],
                send,
                recv,
                w,
                to,
            ).start()
        pltpu.make_async_copy(
            source.at[r, span(x, chunk), :], target.at[r, span(x, chunk), :], recv
        ).start()

    def lev_wait(kind, r, c):
        target = (blocks, returned)[kind]
        drain(target.at[r, all_waves(chunks[kind][r][c]), :], lev_recv.at[kind, r, c])

    def unpack(r, c):
        chunk = chunks[0][r][c]
        first, n = chunk
        lane = lax.broadcasted_iota(jnp.int32, (n, LANES), 1)

        @pl.loop(0, nx)
        def _(lg):
            bands = [
                blocks[r, from_wave(lg * near + b, chunk), :]
                for b in range(near)
            ]
            for i in range(per):
                at = pl.ds(first * cells + lg * per + i, n, stride=cells)
                for t in range(tiles_j):
                    value = None
                    for b in range(near):
                        low = b * band - t * LANES
                        if low + band <= 0 or low >= LANES:
                            continue
                        turn = (low - i * band) % LANES
                        moved = pltpu.roll(bands[b], turn, 1) if turn else bands[b]
                        value = moved if value is None else jnp.where(lane >= low, moved, value)
                    planes_in[t, at, :] = value

    def places(parts, u):
        before = [0, 0]
        for v, (first, count) in enumerate(parts):
            start, m = first * cells, count * cells
            offset, length = start * 5 // 2, m * 5 // 2
            cut = (length // 2 + 7) // 8 * 8
            if v == u:
                return (
                    (start, m, offset),
                    pl.ds(offset, cut),
                    pl.ds(offset + cut, length - cut),
                    pl.ds(before[0], cut),
                    pl.ds(before[1], length - cut),
                )
            before = [before[0] + cut, before[1] + length - cut]

    def analysis(p, u, h):
        s = p % 2
        start, m, offset = places(PARTS_SUM[p], u)[0]
        n_at = pl.ds(pl.multiple_of(h * half_n, 16), half_n)
        a_hi, a_lo = grid_hi[start : start + m, :], grid_lo[start : start + m, :]
        b_hi, b_lo = leg_hi[s, n_at, :], leg_lo[s, n_at, :]
        dot = functools.partial(
            lax.dot_general,
            dimension_numbers=(((1,), (1,)), ((), ())),
            preferred_element_type=f32,
        )
        value = dot(a_hi, b_hi) + (dot(a_hi, b_lo) + dot(a_lo, b_hi))
        low = lax.broadcasted_iota(jnp.int32, (m // 2, LANES), 1) < half
        even, odd = 2 * h, 2 * h + 1
        one, two, three = (pl.ds(offset, m), pl.ds(offset + m, m), pl.ds(offset + 2 * m, m // 2))
        partial[p, even, one, :] = value[:, 0:LANES]
        partial[p, even, two, :] = value[:, LANES : 2 * LANES]
        middle = value[:, 2 * LANES : 3 * LANES]
        first, second = middle[: m // 2], middle[m // 2 :]
        partial[p, even, three, :] = jnp.where(low, first, pltpu.roll(second, half, 1))
        partial[p, odd, three, :] = jnp.where(low, pltpu.roll(first, half, 1), second)
        partial[p, odd, one, :] = value[:, 3 * LANES : 4 * LANES]
        partial[p, odd, two, :] = value[:, 4 * LANES : 5 * LANES]

    def reduce_start(p, u):
        s = p % 2
        (start, m, _), top, bottom, at_a, at_b = places(PARTS_SUM[p], u)
        for t in range(tiles_j):
            value = planes_in[t, s * rows + start : s * rows + start + m, :]
            value = value * mask_weight[s * tiles_j + t : s * tiles_j + t + 1, :]
            high = value.astype(bf16)
            lanes = slice(t * LANES, (t + 1) * LANES)
            grid_hi[start : start + m, lanes] = high
            grid_lo[start : start + m, lanes] = (value - high.astype(f32)).astype(bf16)
        send, recv = sum_send.at[p], sum_recv.at[p, u]
        analysis(p, u, far // 2)
        remote(partial.at[p, far, top], sum_a.at[p, at_a], send, recv.at[0], w, right).start()
        remote(partial.at[p, far, bottom], sum_b.at[p, at_b], send, recv.at[1], w, left).start()
        analysis(p, u, x // 2)
        remote(
            partial.at[p, right, bottom], sum_left.at[p, bottom], send, recv.at[2], w, right
        ).start()
        remote(partial.at[p, left, top], sum_right.at[p, top], send, recv.at[3], w, left).start()

    def reduce_forward(p, u):
        _, top, bottom, at_a, at_b = places(PARTS_SUM[p], u)
        send, recv = sum_send.at[p], sum_recv.at[p, u]
        drain(sum_a.at[p, at_a], recv.at[0])
        partial[p, right, top, :] += sum_a[p, at_a, :]
        remote(partial.at[p, right, top], sum_left.at[p, top], send, recv.at[4], w, right).start()
        drain(sum_b.at[p, at_b], recv.at[1])
        partial[p, left, bottom, :] += sum_b[p, at_b, :]
        remote(
            partial.at[p, left, bottom], sum_right.at[p, bottom], send, recv.at[5], w, left
        ).start()

    def solve(p):
        s = p % 2
        pieces = []
        for u in range(len(PARTS_SUM[p])):
            (_, m, offset), top, bottom, _, _ = places(PARTS_SUM[p], u)
            recv = sum_recv.at[p, u]
            drain(sum_left.at[p, bottom], recv.at[2])
            drain(sum_right.at[p, top], recv.at[3])
            drain(sum_left.at[p, top], recv.at[4])
            drain(sum_right.at[p, bottom], recv.at[5])
            at = pl.ds(offset, m * 5 // 2)
            value = partial[p, x, at, :] + (sum_left[p, at, :] + sum_right[p, at, :])
            last = value[2 * m :]
            pieces.append(
                jnp.concatenate(
                    [
                        value[:m],
                        value[m : 2 * m],
                        jnp.concatenate([last, pltpu.roll(last, half, 1)], axis=0),
                    ],
                    axis=1,
                )
            )
        value = pieces[0] if len(pieces) == 1 else jnp.concatenate(pieces, axis=0)
        lanes = lax.broadcasted_iota(jnp.int32, (1, LANES), 1)
        begin, odd = (x // 2) * half_n, x % 2
        first = begin + odd * (half_n - 2 * LANES) + lanes
        middle = begin + 2 * LANES + odd * half + lanes % half
        n = jnp.concatenate([first, first + LANES, middle], axis=1)
        value = jnp.where(n >= own_zonal(s), value, 0.0)
        factor = (n * (n + 1)).astype(f32) * (4.0 / (total * (total + 1)))
        both = jnp.dot(modal_in[...], value, precision=highest, preferred_element_type=f32)
        diagonal = lax.broadcasted_iota(jnp.int32, (size, size), 0) == lax.broadcasted_iota(
            jnp.int32, (size, size), 1
        )
        depth = jnp.sum(jnp.where(diagonal, eigen[...], 0.0), axis=1, keepdims=True)
        modal = (both[:size] + factor * both[size:]) / (1.0 + depth * factor)
        answer = jnp.dot(modal_out[...], modal, precision=highest, preferred_element_type=f32)
        thermal = lax.broadcasted_iota(jnp.int32, (rows, 1), 0) >= size
        answer = answer + jnp.where(thermal, value, 0.0)
        for u in range(len(PARTS_GATHER[p])):
            start, m, offset = places(PARTS_GATHER[p], u)[0]
            low = lax.broadcasted_iota(jnp.int32, (m // 2, LANES), 1) < half
            part = answer[start : start + m]
            solved[p, x, pl.ds(offset, m), :] = part[:, :LANES]
            solved[p, x, pl.ds(offset + m, m), :] = part[:, LANES : 2 * LANES]
            last = part[:, 2 * LANES :]
            solved[p, x, pl.ds(offset + 2 * m, m // 2), :] = jnp.where(
                low, last[: m // 2], pltpu.roll(last[m // 2 :], half, 1)
            )

    def gather_start(p):
        send = gather_send.at[p]
        for u in range(len(PARTS_GATHER[p])):
            halves = places(PARTS_GATHER[p], u)[1:3]
            for step in range(2):
                for to, first in ((right, 0), (left, 1)):
                    part = (first, 1 - first)[step]
                    block = solved.at[p, x, halves[part]]
                    remote(
                        block, block, send, gather_recv.at[p, u, 2 * first + part], w, to
                    ).start()

    def gather_forward(p, u):
        _, top, bottom, _, _ = places(PARTS_GATHER[p], u)
        send, recv = gather_send.at[p], gather_recv.at[p, u]
        for block, got, index, to in (
            (solved.at[p, left, top], 0, 4, right),
            (solved.at[p, right, bottom], 3, 5, left),
        ):
            drain(block, recv.at[got])
            remote(block, block, send, recv.at[index], w, to).start()

    def gather_wait(p, u):
        _, top, bottom, _, _ = places(PARTS_GATHER[p], u)
        recv = gather_recv.at[p, u]
        drain(solved.at[p, left, bottom], recv.at[1])
        drain(solved.at[p, right, top], recv.at[2])
        drain(solved.at[p, far, top], recv.at[4])
        drain(solved.at[p, far, bottom], recv.at[5])

    def synthesis(p, u):
        s = p % 2
        start, m, offset = places(PARTS_GATHER[p], u)[0]
        low = lax.broadcasted_iota(jnp.int32, (m // 2, LANES), 1) < half
        one, two, three = (pl.ds(offset, m), pl.ds(offset + m, m), pl.ds(offset + 2 * m, m // 2))
        at, upper, lower = (pl.ds(start, m), pl.ds(start, m // 2), pl.ds(start + m // 2, m // 2))
        for h in range(2):
            even, odd, t = 2 * h, 2 * h + 1, h * (tiles_n // 2)
            mixed[t, at, :] = solved[p, even, one, :]
            mixed[t + 1, at, :] = solved[p, even, two, :]
            before, after = solved[p, even, three, :], solved[p, odd, three, :]
            mixed[t + 2, upper, :] = jnp.where(low, before, pltpu.roll(after, half, 1))
            mixed[t + 2, lower, :] = jnp.where(low, pltpu.roll(before, half, 1), after)
            mixed[t + 3, at, :] = solved[p, odd, one, :]
            mixed[t + 4, at, :] = solved[p, odd, two, :]
        for t in range(tiles_n):
            value = mixed[t, at, :]
            high = value.astype(bf16)
            lanes = slice(t * LANES, (t + 1) * LANES)
            spec_hi[start : start + m, lanes] = high
            spec_lo[start : start + m, lanes] = (value - high.astype(f32)).astype(bf16)
        a_hi, a_lo = spec_hi[start : start + m, :], spec_lo[start : start + m, :]
        begin = 0
        while begin < quarter:
            width = min(256, quarter - begin)
            b_hi = leg_hi[s, :, begin : begin + width]
            b_lo = leg_lo[s, :, begin : begin + width]
            dot = functools.partial(jnp.dot, preferred_element_type=f32)
            value = dot(a_hi, b_hi) + (dot(a_hi, b_lo) + dot(a_lo, b_hi))
            for t in range(width // LANES):
                tile = begin // LANES + t
                row = s * tiles_j + tile
                here = mask_present[row : row + 1, :] > 0.5
                planes_out[tile, pl.ds(s * rows + start, m), :] = jnp.where(
                    here, value[:, t * LANES : (t + 1) * LANES], 0.0
                )
            begin += width

    def write_spectral(p, u):
        r, s = p // 2, p % 2
        first, count = PARTS_GATHER[p][u]
        for t in range(tiles_n):
            for i in range(per):
                for k in range(first, first + count):
                    c, third = k // thirds, k % thirds
                    spec_rows[
                        s,
                        per * third + i,
                        2 * c + r : 2 * c + r + 1,
                        t * LANES : (t + 1) * LANES,
                    ] = mixed[t, pl.ds(k * cells + x * per + i, 1), :]

    def pack(r, c):
        chunk = chunks[1][r][c]
        first, n = chunk
        lane = lax.broadcasted_iota(jnp.int32, (n, LANES), 1)

        @pl.loop(0, nx)
        def _(lg):
            tiles = [
                [
                    planes_out[t, pl.ds(first * cells + lg * per + i, n, stride=cells), :]
                    for t in range(tiles_j)
                ]
                for i in range(per)
            ]
            for b in range(near):
                value = None
                for i in range(per):
                    t, low = (b * band) // LANES, (b * band) % LANES
                    turn = (i * band - low) % LANES
                    moved = tiles[i][t]
                    moved = pltpu.roll(moved, turn, 1) if turn else moved
                    if low + band > LANES:
                        other = tiles[i][t + 1]
                        other = pltpu.roll(other, turn, 1) if turn else other
                        moved = jnp.where(lane >= i * band + LANES - low, other, moved)
                    value = moved if value is None else jnp.where(lane >= i * band, moved, value)
                packed[r, from_wave(lg * near + b, chunk), :] = value

    def write_back(r, c):
        at = pl.ds((2 * c + r) * lev * band, lev * band)
        return pltpu.make_async_copy(result.at[at, :], fourier_new.at[at, :], out_sem.at[r, c])

    def collect(r):
        for k in range(pairs):
            for s in range(2):
                at = s * pairs + k
                first, n = next(chunk for chunk in chunks[1][r] if at < sum(chunk))
                square[k % 2, pl.ds(s, nw, stride=2), :] = final[
                    r, pl.ds(nw * first + at - first, nw, stride=n), :
                ]
            result[pl.ds(first_row(r, k), per * band), :] = square[k % 2].T[: per * band]
            if k % thirds == thirds - 1:
                write_back(r, k // thirds).start()

    def split(s):
        leg_copies[s].wait()
        chunk = 64

        @pl.loop(0, total // chunk)
        def _(k):
            at = pl.ds(pl.multiple_of(k * chunk, chunk), chunk)
            value = leg_full[s, at, :]
            high = value.astype(bf16)
            leg_hi[s, at, :] = high
            leg_lo[s, at, :] = (value - high.astype(f32)).astype(bf16)

    def matrices():
        for copy in small_copies:
            copy.wait()
        masks()
        exact = functools.partial(jnp.dot, precision=highest, preferred_element_type=f32)
        modal_in[:size, :] = exact(project[...], pick_div[...])
        modal_in[size:, :] = exact(exact(project[...], balance[...]), pick_temp[...])
        modal_out[...] = exact(place_div[...], modes[...]) - exact(
            place_temp[...], exact(reply[...], modes[...])
        )

    spread(0, 0, chunks[0][0][0][1])
    pl.semaphore_wait(barrier, nw - 1 + nx - 1)
    wave_in(0, 0)
    spread(0, chunks[0][0][0][1], pairs)
    split(0)
    wave_in(0, 1)
    wave_in(0, 2)
    matrices()
    wave_in_wait(0, 0)
    spread(1, 0, pairs)
    lev_start(0, 0, 0)
    wave_in_wait(0, 1)
    lev_start(0, 0, 1)
    wave_in(1, 1)
    wave_in(1, 0)
    lev_wait(0, 0, 0)
    unpack(0, 0)
    reduce_start(0, 0)
    lev_wait(0, 0, 1)
    unpack(0, 1)
    wave_in_wait(0, 2)
    lev_start(0, 0, 2)
    wave_in(1, 2)
    reduce_forward(0, 0)
    reduce_start(0, 1)
    split(1)
    wave_in_wait(1, 1)
    lev_start(0, 1, 1)
    lev_wait(0, 0, 2)
    unpack(0, 2)
    reduce_forward(0, 1)
    reduce_start(1, 0)
    solve(0)
    wave_in_wait(1, 0)
    gather_start(0)
    reduce_forward(1, 0)
    lev_start(0, 1, 0)
    lev_wait(0, 1, 1)
    gather_forward(0, 0)
    wave_in_wait(1, 2)
    unpack(1, 1)
    solve(1)
    lev_start(0, 1, 2)
    gather_start(1)
    gather_wait(0, 0)
    lev_wait(0, 1, 0)
    synthesis(0, 0)
    unpack(1, 0)
    pack(0, 0)
    reduce_start(2, 0)
    gather_forward(1, 0)
    lev_start(1, 0, 0)
    write_spectral(0, 0)
    lev_wait(0, 1, 2)
    unpack(1, 2)
    reduce_start(3, 0)
    gather_wait(1, 0)
    reduce_forward(2, 0)
    lev_wait(1, 0, 0)
    synthesis(1, 0)
    pack(0, 1)
    lev_start(1, 0, 1)
    reduce_forward(3, 0)
    write_spectral(1, 0)
    wave_out(0, 0)
    solve(2)
    pack(0, 2)
    gather_start(2)
    lev_wait(1, 0, 1)
    lev_start(1, 0, 2)
    gather_forward(2, 0)
    solve(3)
    wave_out(0, 1)
    gather_start(3)
    lev_wait(1, 0, 2)
    wave_out(0, 2)
    gather_wait(2, 0)
    synthesis(2, 0)
    gather_forward(3, 0)
    pack(1, 0)
    lev_start(1, 1, 0)
    write_spectral(2, 0)
    gather_wait(3, 0)
    synthesis(3, 0)
    gather_forward(3, 1)
    pack(1, 1)
    lev_start(1, 1, 1)
    lev_wait(1, 1, 0)
    wave_out(1, 0)
    gather_wait(3, 1)
    synthesis(3, 1)
    pack(1, 2)
    lev_start(1, 1, 2)
    lev_wait(1, 1, 1)
    wave_out(1, 1)
    lev_wait(1, 1, 2)
    wave_out(1, 2)
    write_spectral(3, 0)
    write_spectral(3, 1)
    spec_copy = pltpu.make_async_copy(spec_rows, spectral, out_sem.at[0, 2])
    spec_copy.start()
    wave_out_wait(0, 0)
    wave_out_wait(0, 1)
    wave_out_wait(0, 2)
    collect(0)

    for kind in range(2):
        for r in range(2):
            for c, chunk in enumerate(chunks[kind][r]):
                drain(in_rows.at[r, all_waves(chunk, nw - 1), :], wave_send.at[kind, r, c])
                sent = nw - near
                drain(in_rows.at[r, all_waves(chunk, sent), :], lev_send.at[kind, r, c])
    for p in range(4):
        drain(solved.at[p, pl.ds(0, 3)], sum_send.at[p])
        drain(solved.at[p, pl.ds(0, 3)], gather_send.at[p])
    for c in range(len(chunks[1][1])):
        wave_out_wait(1, c)
    collect(1)
    spec_copy.wait()
    for r in range(2):
        for c in range(2):
            write_back(r, c).wait()


def hand_on(parts, spectral_raw, fourier_raw, spectral, fourier_new, low, high, sems):
    rows = fourier_raw.shape[0] // parts
    blocks = [pl.ds(i * rows, rows) for i in range(parts)]
    routes = [
        (fourier_raw.at[at, :], low.at[at, :], fourier_new.at[at, :]) for at in blocks
    ] + [(spectral_raw.at[s], high.at[s], spectral.at[s]) for s in range(spectral.shape[0])]
    arrivals = [
        pltpu.make_async_copy(source, held, sems.at[0, i])
        for i, (source, held, _) in enumerate(routes)
    ]
    departures = [
        pltpu.make_async_copy(held, target, sems.at[1, i])
        for i, (_, held, target) in enumerate(routes)
    ]
    for copy in arrivals:
        copy.start()
    for first, second in zip(arrivals, departures):
        first.wait()
        second.start()
    for copy in departures:
        copy.wait()


def on_device(
    nw,
    nx,
    fourier,
    legendre,
    weights,
    points,
    zonal,
    pressure_balance_matrix,
    modes,
    project,
    eigen,
    thermal_reply_matrix,
):
    waves, parts, lev, band = fourier.shape
    slots, total, quarter = legendre.shape
    size = nx * lev
    per = LANES // band
    groups = parts * lev // per
    rows = 2 * size
    whole = 2 * rows + size
    cut = (whole // 2 + 7) // 8 * 8
    tiles_n = total // LANES
    dims = (nw, nx, band, lev, total, quarter)

    pick = np.zeros((2, size, rows), np.float32)
    row = 0
    for c in range(2):
        for third in range(lev // per):
            for group in range(nx):
                for i in range(per):
                    pick[c, group * lev + per * third + i, row] = 1.0
                    row += 1

    view = fourier.transpose(1, 2, 3, 0).reshape(parts * lev * band, waves)
    f32, bf16 = jnp.float32, jnp.bfloat16
    anywhere = pl.BlockSpec(memory_space=pl.ANY)
    dma = pltpu.SemaphoreType.DMA
    lines = pltpu.VMEM((2, nw * groups, LANES), f32)
    spectral, fourier_new = pl.pallas_call(
        functools.partial(kernel, dims),
        out_shape=(
            jax.ShapeDtypeStruct((slots, lev, parts, total), f32),
            jax.ShapeDtypeStruct(view.shape, f32),
        ),
        in_specs=[anywhere] * 14,
        out_specs=(anywhere, anywhere),
        scratch_shapes=[
            pltpu.VMEM((weights.shape[0] // LANES, LANES), f32),
            pltpu.VMEM((weights.shape[0] // LANES, LANES), jnp.int32),
            pltpu.VMEM((1, waves), jnp.int32),
            pltpu.VMEM((size, size), f32),
            pltpu.VMEM((size, size), f32),
            pltpu.VMEM((size, size), f32),
            pltpu.VMEM((1, size), f32),
            pltpu.VMEM((size, size), f32),
            pltpu.VMEM((size, rows), f32),
            pltpu.VMEM((size, rows), f32),
            pltpu.VMEM((rows, size), f32),
            pltpu.VMEM((rows, size), f32),
            pltpu.VMEM(view.shape, f32),
            pltpu.VMEM((slots, total, quarter), f32),
            pltpu.VMEM((slots, total, quarter), bf16),
            pltpu.VMEM((slots, total, quarter), bf16),
            pltpu.VMEM((2 * (quarter // LANES), LANES), f32),
            pltpu.VMEM((2 * (quarter // LANES), LANES), f32),
            pltpu.VMEM((2, LANES, LANES), f32),
            lines,
            lines,
            lines,
            pltpu.VMEM((quarter // LANES, 2 * rows, LANES), f32),
            pltpu.VMEM((quarter // LANES, 2 * rows, LANES), f32),
            pltpu.VMEM((rows, quarter), bf16),
            pltpu.VMEM((rows, quarter), bf16),
            pltpu.VMEM((4, nx, whole, LANES), f32),
            pltpu.VMEM((4, cut, LANES), f32),
            pltpu.VMEM((4, cut, LANES), f32),
            pltpu.VMEM((4, whole, LANES), f32),
            pltpu.VMEM((4, whole, LANES), f32),
            pltpu.VMEM((rows, rows), f32),
            pltpu.VMEM((rows, size), f32),
            pltpu.VMEM((4, nx, whole, LANES), f32),
            pltpu.VMEM((tiles_n, rows, LANES), f32),
            pltpu.VMEM((rows, total), bf16),
            pltpu.VMEM((rows, total), bf16),
            pltpu.VMEM((slots, lev, parts, total), f32),
            lines,
            lines,
            lines,
            pltpu.VMEM(view.shape, f32),
            dma((12,)),
            dma((2, 2)),
            dma((2,)),
            dma((2, 2, 3)),
            dma((2, 2, 3)),
            dma((2, 2, 3)),
            dma((2, 2, 3)),
            dma((4,)),
            dma((4, 2, 6)),
            dma((4,)),
            dma((4, 2, 6)),
            dma((2, 3)),
        ],
        compiler_params=pltpu.CompilerParams(
            collective_id=0, has_side_effects=True, vmem_limit_bytes=58 * 1024 * 1024
        ),
    )(
        view,
        legendre,
        weights.reshape(-1, LANES),
        points.reshape(-1, LANES),
        zonal.reshape(1, waves),
        pressure_balance_matrix,
        modes,
        project,
        eigen.reshape(1, size),
        thermal_reply_matrix,
        jnp.asarray(pick[0]),
        jnp.asarray(pick[1]),
        jnp.asarray(pick[0].T),
        jnp.asarray(pick[1].T),
    )
    spectral, fourier_new = pl.pallas_call(
        functools.partial(hand_on, 4),
        out_shape=(
            jax.ShapeDtypeStruct(spectral.shape, f32),
            jax.ShapeDtypeStruct(fourier_new.shape, f32),
        ),
        in_specs=[anywhere] * 2,
        out_specs=(anywhere, anywhere),
        scratch_shapes=[
            pltpu.VMEM(fourier_new.shape, f32),
            pltpu.VMEM(spectral.shape, f32),
            dma((2, 4 + slots)),
        ],
    )(spectral, fourier_new)
    spectral = spectral.transpose(0, 2, 1, 3)
    fourier_new = fourier_new.reshape(parts, lev, band, waves).transpose(3, 0, 1, 2)
    return (spectral, fourier_new)


def solution(mesh):
    return jax.shard_map(
        functools.partial(on_device, mesh.shape["wave"], mesh.shape["lev"]),
        mesh=mesh,
        in_specs=(
            P(None, None, "lev", "wave"),
            P("wave", None, "lev"),
            P(),
            P(),
            P(),
            P(),
            P(),
            P(),
            P(),
            P(),
        ),
        out_specs=(P("wave", None, "lev", None), P(None, None, "lev", "wave")),
        check_vma=False,
    )
```
